512 devices in a mesh: seq: 16 (over z_hi, x, core), head: 32 (over z_lo, y).
Axes of the slice: x: 4, y: 8, z: 8 (z_hi: 2, z_lo: 4; z = z_hi * 4 + z_lo), core: 2. Of those that a mesh axis runs over, the one named last changes fastest.
Arguments:
- queries: bfloat16 [4096, 16384], P('seq', 'head'), may hold values from -100 to 100
- key_rows: bfloat16 [4096, 1024], P('seq'), may hold values from -4 to 4
- value_rows: bfloat16 [4096, 1024], P('seq'), may hold values from -6 to 6
- value_turn: bfloat16 [8, 128, 128], replicated, may hold values from -0.5 to 0.5
- block_map: int32 [128], replicated, may hold values from 0 to 127, each once
- block_turn: bfloat16 [128, 128, 128], P('head'), may hold values from -0.5 to 0.5
- out_weight: bfloat16 [16384, 8192], P('head', 'seq'), may hold values from -1.5 to 1.5
Outputs:
- mixed: bfloat16 [8192, 4096], P('head', 'seq')
The draws below stay inside these ranges and needn't reach their ends.
Inputs may be any that keep to these rules, and one draw needn't show every extreme that they name: `block_map`: every block position 0 to 127 appears once.
All inputs are finite; a program needn't handle non-finite values.
Results may differ from the reference program's by a relative error of at most 0.03.
Values may be sent and summed in bfloat16 or wider, within the bound.
A program may use at most 128 MiB of HBM per device.

```python
import jax
import jax.numpy as jnp
from jax import lax

HD = 128
GROUP = 16
HEAD_DEV = 4
OUT = 8192
HEADS = 128
KVH = 8
TOKENS = 4096


def common_keys(key):
    base = jax.random.normal(key, (TOKENS, KVH * HD), jnp.float32)
    return jnp.clip(base, -4.0, 4.0)


def draw_key_rows(key, part):
    keys_now = common_keys(key)
    return keys_now.astype(jnp.bfloat16)


def draw_queries(key, part):
    key = jax.random.fold_in(key, 7)
    base = jnp.clip(jax.random.normal(key, (TOKENS, HEADS * HD), jnp.float32), -4.0, 4.0)
    return base.astype(jnp.bfloat16)


def raised(entries, stream_key, source, target, blocks, factor):
    def block_of(dim):
        return (jnp.arange(entries.shape[dim]) // (entries.shape[dim] // blocks)).reshape((-1,) + (1,) * (entries.ndim - 1 - dim))

    one_side = jax.random.permutation(stream_key, blocks)[block_of(target)]
    second = (block_of(target) + blocks // 2) % blocks
    return jnp.where((block_of(source) == one_side) | (block_of(source) == second), factor * entries, entries)


def level_of(key, shape, split, least, top_value):
    loudness = 1.0
    for axis_at, blocks in split:
        draws = jax.random.uniform(jax.random.fold_in(jax.random.fold_in(key, 6), axis_at), (blocks,), jnp.float32, least / len(split), top_value / len(split))
        loudness = loudness * jnp.repeat(jnp.exp(draws), shape[axis_at] // blocks).reshape((-1,) + (1,) * (len(shape) - 1 - axis_at))
    return loudness


def scatter_about(stream_key, dims, deviation, most, pieces=(), held_as=jnp.bfloat16):
    array = deviation * jax.random.normal(stream_key, dims, jnp.float32)
    if pieces:
        array = array * level_of(stream_key, dims, pieces, -0.22, 0.18)
    return jnp.clip(array, -most, most).astype(held_as)


def noise_with(key, shape, spread, reach, pieces, heavy, kind=jnp.bfloat16):
    drawn = spread * jax.random.normal(key, shape, jnp.float32)
    if pieces:
        drawn = drawn * level_of(key, shape, pieces, -0.22, 0.18)
    return jnp.clip(raised(drawn, jax.random.fold_in(key, 3), *heavy), -reach, reach).astype(kind)


def setup_inputs(seed: int = 0) -> dict:
    splits = jax.random.split(jax.random.key(seed), 8)
    queries = draw_queries(jax.random.fold_in(splits[7], 71), 0)
    key_rows = draw_key_rows(jax.random.fold_in(splits[7], 71), 0)
    value_rows = scatter_about(splits[2], (TOKENS, KVH * HD), 1.0, 6.0, ((0, 16),))
    value_turn = scatter_about(splits[3], (KVH, HD, HD), HD ** -0.5, 0.5)
    block_map = jax.random.permutation(splits[4], HEADS).astype(jnp.int32)
    block_turn = scatter_about(splits[5], (HEADS, HD, HD), HD ** -0.5, 0.5, ((0, 32),))
    out_weight = noise_with(splits[6], (HEADS * HD, OUT), (HEADS * HD // 256) ** -0.5, 1.5, ((0, 32), (1, 16)), (0, 1, 32, 2.75))
    return dict(queries=queries, key_rows=key_rows, value_rows=value_rows, value_turn=value_turn, block_map=block_map, block_turn=block_turn, out_weight=out_weight)


def attend_one(query_head, key_head, value_head, allowed, scale):
    scores = jnp.dot(query_head, key_head.T, preferred_element_type=jnp.float32) * scale
    masked = jnp.where(allowed, scores, jnp.float32(-1e30))
    top = jnp.max(masked, axis=1)
    weights = jnp.where(allowed, jnp.exp(scores - top[:, None]), jnp.float32(0.0))
    total = jnp.sum(weights, axis=1)
    summed = jnp.dot(weights.astype(jnp.bfloat16), value_head, preferred_element_type=jnp.float32)
    return (summed / total[:, None]).astype(jnp.bfloat16)


def reference(queries, key_rows, value_rows, value_turn, block_map, block_turn, out_weight):
    scale = 1.0 / (HD ** 0.5)
    value_three = value_rows.reshape(TOKENS, KVH, HD).astype(jnp.float32)
    turned_values = jnp.einsum("tgc,gcd->tgd", value_three, value_turn.astype(jnp.float32)).astype(jnp.bfloat16)
    key_three = key_rows.reshape(TOKENS, KVH, HD)
    query_three = queries.reshape(TOKENS, HEADS, HD)
    positions = jnp.arange(TOKENS, dtype=jnp.int32)
    allowed = positions[None, :] <= positions[:, None]

    def per_head(head):
        group = head // GROUP
        query_head = lax.dynamic_index_in_dim(query_three, head, 1, keepdims=False)
        key_head = lax.dynamic_index_in_dim(key_three, group, 1, keepdims=False)
        value_head = lax.dynamic_index_in_dim(turned_values, group, 1, keepdims=False)
        return attend_one(query_head, key_head, value_head, allowed, scale)

    attended = lax.map(per_head, jnp.arange(HEADS, dtype=jnp.int32))
    attended = jnp.transpose(attended, (1, 0, 2))
    permuted = jnp.zeros_like(attended).at[:, block_map, :].set(attended)
    rotated = jnp.einsum("tbc,bcd->tbd", permuted.astype(jnp.float32), block_turn.astype(jnp.float32)).astype(jnp.bfloat16)
    groups = HEADS // HEAD_DEV
    rotated_groups = jnp.transpose(rotated.reshape(TOKENS, groups, HEAD_DEV * HD), (1, 0, 2))
    weight_groups = out_weight.reshape(groups, HEAD_DEV * HD, OUT)

    def add_group(carry, pair):
        left, right = pair
        partial_value = jnp.dot(left, right, preferred_element_type=jnp.float32).astype(jnp.bfloat16)
        return carry + partial_value.astype(jnp.float32), None

    summed, _ = lax.scan(add_group, jnp.zeros((TOKENS, OUT), jnp.float32), (rotated_groups, weight_groups))
    return summed.T.astype(jnp.bfloat16)
```

```python
import functools
import math

import jax
import jax.numpy as jnp
from jax import lax
from jax.experimental import pallas as pl
from jax.experimental.pallas import tpu as pltpu
from jax.sharding import PartitionSpec as P

MESH = pl.DeviceIdType.MESH
BF = jnp.bfloat16
F32 = jnp.float32
HD = 128
TOK = 256


def dev(zh, x, c, zl, y):
    return (zh * 8 + x * 2 + c, zl * 8 + y)


def send(src, dst, ssem, rsem, to):
    copy = pltpu.make_async_remote_copy(
        src_ref=src, dst_ref=dst, send_sem=ssem, recv_sem=rsem, device_id=to, device_id_type=MESH
    )
    copy.start()
    return copy


def arrived(slot, sem):
    pltpu.make_async_copy(slot, slot, sem).wait()


def kernel(
    map_ref, q_ref, key_ref, val_ref, vturn_ref, bturn_ref, w_ref, out_ref,
    kv, q_all, score, att, wst, w1, w2s, wfull, a_st, a_full, cst, cin,
    kc_s, kx_s, kx_r, kc_r, kd_s, kd_r, kxx_s, kxx_r,
    w1_s, w1_r, w2_s, w2_r, wx_s, wx_r, wd_s, wd_r,
    ac_s, ac_r, rr_s, rr_r, ll_s, ll_r, c_s, c_r,
):
    s = lax.axis_index("seq")
    h = lax.axis_index("head")
    zh, x, c = s // 8, (s // 2) % 4, s % 2
    zl, y = h // 8, h % 8
    z = zh * 4 + zl

    g = zl * 2 + y // 4
    lanes = pl.ds(pl.multiple_of(g * HD, HD), HD)
    kv[s, 0] = key_ref[:, lanes]
    kv[s, 1] = jnp.dot(val_ref[:, lanes], vturn_ref[g], preferred_element_type=F32).astype(BF)

    @pl.when(zh == 0)
    def _():
        send(kv.at[s], kv.at[s], kc_s, kc_r, dev(1, x, c, zl, y))

    for off in (1, 2, 3):
        @pl.when(x + off < 4)
        def _():
            send(kv.at[s], kv.at[s], kx_s.at[off], kx_r.at[x], dev(zh, x + off, c, zl, y))

    @pl.when(c == 0)
    def _():
        send(kv.at[s], kv.at[s], kd_s.at[zh * 4 + x], kd_r.at[zh * 4 + x], dev(zh, x, 1, zl, y))

    for i in range(4):
        turned = lax.dot_general(
            w_ref[i * HD:(i + 1) * HD, :], bturn_ref[i], (((0,), (1,)), ((), ())), preferred_element_type=F32
        ).astype(BF)
        wst[:, i] = turned.reshape(32, 16, HD)
    x_to = (x + zh) % 4

    def w1_place(n):
        r, m = n // 16, n % 16
        cq, zq = m // 8, m % 8
        return dev(zq // 4, x_to, cq, zq % 4, 4 * (x % 2) + 2 * c + r)

    def w1_send(step, carry):
        n = (step + h) % 32
        to = w1_place(n)
        mine = (to[0] == s) & (to[1] == h)

        @pl.when(jnp.logical_not(mine))
        def _():
            send(wst.at[n], w1.at[pl.ds(h * 4, 4)], w1_s.at[n], w1_r.at[h], to)

        @pl.when(mine)
        def _():
            pltpu.make_async_copy(wst.at[n], w1.at[pl.ds(h * 4, 4)], w1_r.at[h]).start()

        return carry

    lax.fori_loop(0, 32, w1_send, 0)

    @pl.when(zh == 1)
    def _():
        arrived(kv.at[s - 8], kc_r)
        for off in (1, 2, 3):
            send(kv.at[s - 8], kv.at[s - 8], kxx_s.at[off], kxx_r.at[off], dev(1, (x + off) % 4, c, zl, y))
        send(kv.at[s - 8], kv.at[s - 8], kd_s.at[x], kd_r.at[x], dev(1, x, 1 - c, zl, y))

    for xs in range(3):
        @pl.when(xs < x)
        def _():
            slot = kv.at[zh * 8 + xs * 2 + c]
            arrived(slot, kx_r.at[xs])
            send(slot, slot, kd_s.at[zh * 4 + xs], kd_r.at[zh * 4 + xs], dev(zh, x, 1 - c, zl, y))

    @pl.when(zh == 1)
    def _():
        for off in (1, 2, 3):
            xs = (x + 4 - off) % 4
            slot = kv.at[xs * 2 + c]
            arrived(slot, kxx_r.at[off])
            send(slot, slot, kd_s.at[xs], kd_r.at[xs], dev(1, x, 1 - c, zl, y))

    for hh in range(32):
        arrived(w1.at[pl.ds(hh * 4, 4)], w1_r.at[hh])

    def held_rows(xx):
        zs = (xx + y // 4) % 2
        xs = (xx + 4 - zs) % 4
        return pl.multiple_of((2 * zs + xs // 2) * 256 + c * 128, 128)

    rows = held_rows(x)
    my_rows = pl.ds(pl.multiple_of(rows + z * 16, 16), 16)

    def w2_send(step, carry):
        zt = (z + step) % 8
        zht, zlt = zt // 4, zt % 4
        for kk in range(16):
            block = map_ref[(zlt * 8 + kk // 2) * 4 + zht * 2 + kk % 2]
            w2s[step, :, kk * HD:(kk + 1) * HD] = w1[block]

        @pl.when(step > 0)
        def _():
            send(w2s.at[step], wfull.at[my_rows, :], w2_s.at[step], w2_r.at[z], dev(zht, x, c, zlt, y))

        @pl.when(step == 0)
        def _():
            pltpu.make_async_copy(w2s.at[step], wfull.at[my_rows, :], w2_r.at[z]).start()

        return carry

    lax.fori_loop(0, 8, w2_send, 0)

    for xs in range(4):
        @pl.when((xs < x) | ((xs == x) & (c == 1)))
        def _():
            arrived(kv.at[zh * 8 + xs * 2 + 1 - c], kd_r.at[zh * 4 + xs])

        @pl.when(zh == 1)
        def _():
            arrived(kv.at[xs * 2 + 1 - c], kd_r.at[xs])

    for i in range(4):
        q_all[i * TOK:(i + 1) * TOK, :] = q_ref[:, i * HD:(i + 1) * HD]
    turn = math.log2(math.e) / math.sqrt(HD)

    def scored(i, u):
        return lax.dot_general(
            q_all[i * TOK:(i + 1) * TOK, :], kv[u, 0], (((1,), (1,)), ((), ())), preferred_element_type=F32
        )

    seen = lax.broadcasted_iota(jnp.int32, (TOK, TOK), 1) <= lax.broadcasted_iota(jnp.int32, (TOK, TOK), 0)
    for i in range(4):
        own = jnp.where(seen, scored(i, s), F32(-1e30))
        score[s] = own

        def first(u, top, i=i):
            value = scored(i, u)
            score[u] = value
            return jnp.maximum(top, jnp.maximum(value[:, :HD], value[:, HD:]))

        top = lax.fori_loop(0, s, first, jnp.maximum(own[:, :HD], own[:, HD:]))
        top = jnp.max(top, axis=1, keepdims=True) * turn

        def second(u, carry, top=top):
            total, acc = carry
            weight = jnp.exp2(score[u] * turn - top)
            total = total + weight[:, :HD] + weight[:, HD:]
            acc = acc + jnp.dot(weight.astype(BF), kv[u, 1], preferred_element_type=F32)
            return total, acc

        zero = jnp.zeros((TOK, HD), F32)
        total, acc = lax.fori_loop(0, s + 1, second, (zero, zero))
        att[i // 2, :, (i % 2) * HD:(i % 2 + 1) * HD] = (acc / jnp.sum(total, axis=1, keepdims=True)).astype(BF)

    a_full[y, zh] = att[zh]
    a_st[...] = att[1 - zh]
    send(a_st, a_full.at[y, zh], ac_s, ac_r, dev(1 - zh, x, c, zl, y))
    right = dev(zh, x, c, zl, (y + 1) % 8)
    left = dev(zh, x, c, zl, (y + 7) % 8)

    def part(slot, p):
        return a_full.at[slot % 8, zh if p == 0 else 1 - zh]

    def go(k, p):
        if k < 3 or p == 0:
            ref = part(y + 8 - k, p)
            send(ref, ref, rr_s.at[k, p], rr_r.at[k, p], right)
        if k < 3 or p == 1:
            ref = part(y + k, p)
            send(ref, ref, ll_s.at[k, p], ll_r.at[k, p], left)

    go(0, 0)

    for zq in range(8):
        arrived(wfull.at[pl.ds(pl.multiple_of(rows + zq * 16, 16), 16), :], w2_r.at[zq])
    chunk = wfull.at[pl.ds(rows, 128), :]
    for off in (1, 2, 3):
        send(chunk, chunk, wx_s.at[off], wx_r.at[off], dev(zh, (x + off) % 4, c, zl, y))
    send(chunk, chunk, wd_s.at[0], wd_r.at[0], dev(zh, x, 1 - c, zl, y))

    arrived(part(y, 1), ac_r)
    go(0, 1)
    for k in (1, 2, 3):
        for p in (0, 1):
            arrived(part(y + 8 - k, p), rr_r.at[k - 1, p])
            arrived(part(y + k, p), ll_r.at[k - 1, p])
            go(k, p)

    for off in (1, 3, 2):
        theirs = wfull.at[pl.ds(held_rows((x + 4 - off) % 4), 128), :]
        arrived(theirs, wx_r.at[off])
        send(theirs, theirs, wd_s.at[off], wd_r.at[off], dev(zh, x, 1 - c, zl, y))
    for off in (0, 1, 3, 2):
        other = held_rows((x + 4 - off) % 4) + 128 - 256 * c
        arrived(wfull.at[pl.ds(pl.multiple_of(other, 128), 128), :], wd_r.at[off])

    arrived(part(y + 4, 0), rr_r.at[3, 0])
    arrived(part(y + 4, 1), ll_r.at[3, 1])

    def piece(step, carry):
        half = (step + 1) // 2
        d = jnp.where(step % 2 == 1, 4 + half, 12 - half) % 8
        zt = (z + d) % 8
        zht, zlt = zt // 4, zt % 4
        cols = pl.ds(pl.multiple_of(zlt * 256, 256), 256)
        acc = jnp.zeros((256, TOK), F32)
        for yy in range(8):
            acc = acc + lax.dot_general(
                wfull[cols, yy * 256:(yy + 1) * 256], a_full[yy, zht], (((1,), (1,)), ((), ())),
                preferred_element_type=F32,
            )

        @pl.when(d > 0)
        def _():
            cst[d] = acc.astype(BF)
            send(cst.at[d], cin.at[z], c_s.at[d], c_r.at[z], dev(zht, x, c, zlt, y))

        @pl.when(d == 0)
        def _():
            cst[0] = acc.astype(BF)

        return carry

    lax.fori_loop(0, 8, piece, 0)
    total = cst[0].astype(F32)
    for d in range(1, 8):
        zs = (z + d) % 8
        arrived(cin.at[zs], c_r.at[zs])
        total = total + cin[zs].astype(F32)
    out_ref[...] = total.astype(BF)

    @pl.when(zh == 0)
    def _():
        arrived(kv.at[s], kc_s)

    for off in (1, 2, 3):
        @pl.when(x + off < 4)
        def _():
            arrived(kv.at[s], kx_s.at[off])

        @pl.when(zh == 1)
        def _():
            arrived(kv.at[s - 8], kxx_s.at[off])

    for xs in range(4):
        @pl.when((xs < x) | ((xs == x) & (c == 0)))
        def _():
            arrived(kv.at[s], kd_s.at[zh * 4 + xs])

        @pl.when(zh == 1)
        def _():
            arrived(kv.at[s], kd_s.at[xs])

    def w1_sent(n, carry):
        to = w1_place(n)

        @pl.when(jnp.logical_not((to[0] == s) & (to[1] == h)))
        def _():
            arrived(wst.at[n], w1_s.at[n])

        return carry

    lax.fori_loop(0, 32, w1_sent, 0)
    for d in range(1, 8):
        arrived(w2s.at[d], w2_s.at[d])
        arrived(cst.at[d], c_s.at[d])
    for off in (1, 2, 3):
        arrived(chunk, wx_s.at[off])
    for off in range(4):
        arrived(chunk, wd_s.at[off])
    arrived(a_st, ac_s)
    for k in range(4):
        for p in (0, 1):
            if k < 3 or p == 0:
                arrived(part(y, 0), rr_s.at[k, p])
            if k < 3 or p == 1:
                arrived(part(y, 0), ll_s.at[k, p])


def on_device(queries, key_rows, value_rows, value_turn, block_map, block_turn, out_weight):
    vmem = pl.BlockSpec(memory_space=pltpu.VMEM)
    dma = pltpu.SemaphoreType.DMA
    return pl.pallas_call(
        kernel,
        out_shape=jax.ShapeDtypeStruct((256, TOK), BF),
        in_specs=[pl.BlockSpec(memory_space=pltpu.SMEM)] + [vmem] * 6,
        out_specs=vmem,
        scratch_shapes=[
            pltpu.VMEM((16, 2, TOK, HD), BF),
            pltpu.VMEM((4 * TOK, HD), BF),
            pltpu.VMEM((16, TOK, TOK), F32),
            pltpu.VMEM((2, TOK, 256), BF),
            pltpu.VMEM((32, 4, 16, HD), BF),
            pltpu.VMEM((128, 16, HD), BF),
            pltpu.VMEM((8, 16, 2048), BF),
            pltpu.VMEM((1024, 2048), BF),
            pltpu.VMEM((TOK, 256), BF),
            pltpu.VMEM((8, 2, TOK, 256), BF),
            pltpu.VMEM((8, 256, TOK), BF),
            pltpu.VMEM((8, 256, TOK), BF),
            dma(()), dma((4,)), dma((4,)), dma(()), dma((8,)), dma((8,)), dma((4,)), dma((4,)),
            dma((32,)), dma((32,)), dma((8,)), dma((8,)), dma((4,)), dma((4,)), dma((4,)), dma((4,)),
            dma(()), dma(()), dma((4, 2)), dma((4, 2)), dma((4, 2)), dma((4, 2)), dma((8,)), dma((8,)),
        ],
        compiler_params=pltpu.CompilerParams(has_side_effects=True, vmem_limit_bytes=48 * 1024 * 1024),
    )(block_map, queries, key_rows, value_rows, value_turn, block_turn, out_weight)


def solution(mesh):
    placed = (
        P("seq", "head"),
        P("seq", None),
        P("seq", None),
        P(),
        P(),
        P("head", None, None),
        P("head", "seq"),
    )
    return jax.shard_map(
        on_device, mesh=mesh, in_specs=placed, out_specs=P("head", "seq"), check_vma=False
    )
```

```python
import math

import jax
import jax.numpy as jnp
from jax import lax
from jax.experimental import pallas as pl
from jax.experimental.pallas import tpu as pltpu
from jax.sharding import PartitionSpec as P

MESH = pl.DeviceIdType.MESH
BF = jnp.bfloat16
F32 = jnp.float32
HD = 128
TOK = 256
HALF = 128


def dev(zh, x, c, zl, y):
    return (zh * 8 + x * 2 + c, zl * 8 + y)


def send(src, dst, ssem, rsem, to):
    pltpu.make_async_remote_copy(
        src_ref=src, dst_ref=dst, send_sem=ssem, recv_sem=rsem, device_id=to, device_id_type=MESH
    ).start()


def arrived(slot, sem):
    pltpu.make_async_copy(slot, slot, sem).wait()


def kernel(
    map_ref, q_ref, key_ref, val_ref, vturn_ref, bturn_ref, w_ref, out_ref,
    kv, q_all, score, top_ref, total_ref, acc_ref, wst, whop, w1, w2s, wfull, a_st, a_full, cst, cin,
    val_in, vturn_in, w_in, bturn_in, q_in, in_s,
    kc_s, kx_s, kx_r, kc_r, kd_s, kd_r, kxx_s, kxx_r,
    wh_s, wh_r, w1_s, w1_r, w2_s, w2_r, wx_s, wx_r, wd_s, wd_r,
    ac_s, ac_r, rr_s, rr_r, ll_s, ll_r, c_s, c_r,
):
    s = lax.axis_index("seq")
    h = lax.axis_index("head")
    zh, x, c = s // 8, (s // 2) % 4, s % 2
    zl, y = h // 8, h % 8
    z = zh * 4 + zl

    g = zl * 2 + y // 4
    lanes = pl.ds(pl.multiple_of(g * HD, HD), HD)
    load_key = pltpu.make_async_copy(key_ref.at[:, lanes], kv.at[s, 0], in_s.at[0])
    load_val = pltpu.make_async_copy(val_ref.at[:, lanes], val_in, in_s.at[1])
    load_vturn = pltpu.make_async_copy(vturn_ref.at[g], vturn_in, in_s.at[2])
    load_w = pltpu.make_async_copy(w_ref, w_in, in_s.at[3])
    load_bturn = pltpu.make_async_copy(bturn_ref, bturn_in, in_s.at[4])
    load_q = pltpu.make_async_copy(q_ref, q_in, in_s.at[5])
    for load in (load_key, load_val, load_vturn, load_w, load_bturn, load_q):
        load.start()

    w_seq = c * 8 + x * 2 + (y // 2) % 2

    def held_rows(xx, cc):
        hf = (xx + y // 4) % 2
        xs = (xx + 4 - hf) % 4
        return pl.multiple_of((2 * cc + xs // 2) * 256 + hf * 128, 128)

    rows = held_rows(x, c)

    def row16(zq):
        return pl.ds(pl.multiple_of(rows + zq * 16, 16), 16)

    def w1_place(n):
        hf, r, zq = n // 16, (n // 8) % 2, n % 8
        return dev(zq // 4, x, zh, zq % 4, 4 * ((x + hf) % 2) + 2 * c + r)

    chunk = wfull.at[pl.ds(rows, 128), :]
    right = dev(zh, x, c, zl, (y + 1) % 8)
    left = dev(zh, x, c, zl, (y + 7) % 8)

    barrier = pltpu.get_barrier_semaphore()

    def greet(to):
        pl.semaphore_signal(barrier, inc=1, device_id=to, device_id_type=MESH)

    def greet_w1(hh, carry):
        @pl.when(jnp.logical_not((w_seq == s) & (hh == h)))
        def _():
            greet((w_seq, hh))

        return carry

    def entry():
        for d in range(1, 8):
            zt = (z + d) % 8
            greet(dev(zt // 4, x, c, zt % 4, y))
        for off in (1, 2, 3):
            greet(dev(zh, (x + off) % 4, c, zl, y))
        greet(dev(zh, x, 1 - c, zl, y))
        greet(right)
        greet(left)
        lax.fori_loop(0, 32, greet_w1, 0)

    def all_in():
        self_too = (w_seq == s).astype(jnp.int32)
        pl.semaphore_wait(barrier, 45 - self_too)

    def kv_first():
        load_key.wait()
        load_val.wait()
        load_vturn.wait()
        kv[s, 1] = jnp.dot(val_in[...], vturn_in[...], preferred_element_type=F32).astype(BF)

    def kv_send():
        @pl.when(zh == 0)
        def _():
            send(kv.at[s], kv.at[s], kc_s, kc_r, dev(1, x, c, zl, y))

        for off in (1, 2, 3):
            @pl.when(x + off < 4)
            def _():
                send(kv.at[s], kv.at[s], kx_s.at[off], kx_r.at[x], dev(zh, x + off, c, zl, y))

        send(kv.at[s], kv.at[s], kd_s.at[zh * 4 + x], kd_r.at[zh * 4 + x], dev(zh, x, 1 - c, zl, y))

    def w_turn():
        load_w.wait()
        load_bturn.wait()
        for i in range(4):
            turned = lax.dot_general(
                w_in[i * HD:(i + 1) * HD, :], bturn_in[i], (((0,), (1,)), ((), ())), preferred_element_type=F32
            ).astype(BF)
            turned = turned.reshape(32, 16, HD)
            for r in range(2):
                for hf in range(2):
                    wst[hf * 16 + r * 8:hf * 16 + r * 8 + 8, i] = turned[(r * 2 + hf) * 8:(r * 2 + hf) * 8 + 8]

    def w_hop():
        far = wst.at[pl.ds(16, 16)]
        send(far, whop, wh_s, wh_r, dev(zh, (x + 1) % 4, c, zl, y))

    def w1_send(n, src):
        to = w1_place(n)
        mine = (to[0] == s) & (to[1] == h)

        @pl.when(jnp.logical_not(mine))
        def _():
            send(src, w1.at[pl.ds(h * 4, 4)], w1_s.at[n], w1_r.at[h], to)

        @pl.when(mine)
        def _():
            pltpu.make_async_copy(src, w1.at[pl.ds(h * 4, 4)], w1_r.at[h]).start()

    def w_spread():
        def one(step, carry):
            n = (step + h) % 16
            w1_send(n, wst.at[n])
            return carry

        lax.fori_loop(0, 16, one, 0)

    def w_spread_far():
        arrived(whop, wh_r)

        def one(step, carry):
            n = (step + h) % 16
            w1_send(16 + n, whop.at[n])
            return carry

        lax.fori_loop(0, 16, one, 0)

    def kv_second():
        @pl.when(zh == 1)
        def _():
            arrived(kv.at[s - 8], kc_r)
            for off in (1, 3, 2):
                send(kv.at[s - 8], kv.at[s - 8], kxx_s.at[off], kxx_r.at[off], dev(1, (x + off) % 4, c, zl, y))
            send(kv.at[s - 8], kv.at[s - 8], kd_s.at[x], kd_r.at[x], dev(1, x, 1 - c, zl, y))

        for xs in range(3):
            @pl.when(xs < x)
            def _():
                slot = kv.at[zh * 8 + xs * 2 + c]
                arrived(slot, kx_r.at[xs])
                send(slot, slot, kd_s.at[zh * 4 + xs], kd_r.at[zh * 4 + xs], dev(zh, x, 1 - c, zl, y))

        @pl.when(zh == 1)
        def _():
            for off in (1, 3, 2):
                xs = (x + 4 - off) % 4
                slot = kv.at[xs * 2 + c]
                arrived(slot, kxx_r.at[off])
                send(slot, slot, kd_s.at[xs], kd_r.at[xs], dev(1, x, 1 - c, zl, y))

    def kv_wait():
        for xs in range(4):
            @pl.when(xs <= x)
            def _():
                arrived(kv.at[zh * 8 + xs * 2 + 1 - c], kd_r.at[zh * 4 + xs])

            @pl.when(zh == 1)
            def _():
                arrived(kv.at[xs * 2 + 1 - c], kd_r.at[xs])

    def w2_send(step, carry):
        zt = (z + step) % 8
        zht, zlt = zt // 4, zt % 4
        for kk in range(16):
            block = map_ref[(zlt * 8 + kk // 2) * 4 + zht * 2 + kk % 2]
            w2s[step, :, kk * HD:(kk + 1) * HD] = w1[block]

        @pl.when(step > 0)
        def _():
            send(w2s.at[step], wfull.at[row16(z), :], w2_s.at[step], w2_r.at[z], dev(zht, x, c, zlt, y))

        @pl.when(step == 0)
        def _():
            pltpu.make_async_copy(w2s.at[step], wfull.at[row16(z), :], w2_r.at[z]).start()

        return carry

    def w_pick():
        for hh in range(32):
            arrived(w1.at[pl.ds(hh * 4, 4)], w1_r.at[hh])
        lax.fori_loop(0, 8, w2_send, 0)

    def w_gather():
        for d in (0, 1, 7, 2, 6, 3, 5, 4):
            zq = (z + d) % 8
            piece = wfull.at[row16(zq), :]
            arrived(piece, w2_r.at[zq])
            for off in (1, 3):
                send(piece, piece, wx_s.at[off, zq], wx_r.at[off, zq], dev(zh, (x + off) % 4, c, zl, y))
        send(chunk, chunk, wd_s.at[0], wd_r.at[0], dev(zh, x, 1 - c, zl, y))

    def w_share(off):
        base = held_rows((x + 4 - off) % 4, c)
        for zq in range(8):
            piece = wfull.at[pl.ds(pl.multiple_of(base + zq * 16, 16), 16), :]
            arrived(piece, wx_r.at[off, zq])
            if off == 1 and zq < 4 or off == 3 and zq >= 4:
                onward = dev(zh, (x + off) % 4, c, zl, y)
                send(piece, piece, wx_s.at[2, zq], wx_r.at[2, zq], onward)
        theirs = wfull.at[pl.ds(base, 128), :]
        send(theirs, theirs, wd_s.at[off], wd_r.at[off], dev(zh, x, 1 - c, zl, y))

    def w_shared(off):
        base = held_rows((x + 4 - off) % 4, 1 - c)
        arrived(wfull.at[pl.ds(base, 128), :], wd_r.at[off])

    turn = math.log2(math.e) / math.sqrt(HD)
    last = zh * 4 + x

    def attention(t):
        def scored(i, u, j):
            return lax.dot_general(
                q_all[t, i], kv[2 * u + j, 0], (((1,), (1,)), ((), ())), preferred_element_type=F32
            )

        if t == 0:
            load_q.wait()
        for i in range(4):
            q_all[t, i] = q_in[t * HALF:(t + 1) * HALF, i * HD:(i + 1) * HD]
        place = lax.broadcasted_iota(jnp.int32, (HALF, TOK), 0) + (c * TOK + t * HALF)
        key_at = lax.broadcasted_iota(jnp.int32, (HALF, TOK), 1)
        for i in range(4):
            top = None
            for j in range(2):
                value = jnp.where(key_at + j * TOK <= place, scored(i, last, j), F32(-1e30))
                score[last, i, :, j * TOK:(j + 1) * TOK] = value
                value = jnp.maximum(value[:, :HD], value[:, HD:])
                top = value if top is None else jnp.maximum(top, value)
            top_ref[i] = top

        def first(u, carry):
            for i in range(4):
                top = top_ref[i]
                for j in range(2):
                    value = scored(i, u, j)
                    score[u, i, :, j * TOK:(j + 1) * TOK] = value
                    top = jnp.maximum(top, jnp.maximum(value[:, :HD], value[:, HD:]))
                top_ref[i] = top
            return carry

        lax.fori_loop(0, last, first, 0)
        for i in range(4):
            top_ref[i] = jnp.broadcast_to(jnp.max(top_ref[i], axis=1, keepdims=True) * turn, (HALF, HD))
        total_ref[...] = jnp.zeros_like(total_ref)
        acc_ref[...] = jnp.zeros_like(acc_ref)

        def second(u, carry):
            for i in range(4):
                top = top_ref[i]
                total = total_ref[i]
                acc = acc_ref[i]
                for j in range(2):
                    weight = []
                    for k in range(2):
                        lane = j * TOK + k * HD
                        weight.append(jnp.exp2(score[u, i, :, lane:lane + HD] * turn - top))
                        total = total + weight[k]
                    acc = acc + jnp.dot(
                        jnp.concatenate(weight, axis=1).astype(BF), kv[2 * u + j, 1], preferred_element_type=F32
                    )
                total_ref[i] = total
                acc_ref[i] = acc
            return carry

        lax.fori_loop(0, last + 1, second, 0)

        def head(i):
            return (acc_ref[i] / jnp.sum(total_ref[i], axis=1, keepdims=True)).astype(BF)

        for k in range(2):
            @pl.when(zh == k)
            def _():
                for i in range(2):
                    a_full[t, y, zh, :, i * HD:(i + 1) * HD] = head(2 * k + i)
                    a_st[t, :, i * HD:(i + 1) * HD] = head(2 * (1 - k) + i)

    def part(t, slot, p):
        return a_full.at[t, slot % 8, zh if p == 0 else 1 - zh]

    def go(t, k, p):
        if k < 3 or p == 0:
            ref = part(t, y + 8 - k, p)
            send(ref, ref, rr_s.at[t, k, p], rr_r.at[t, k, p], right)
        if k < 3 or p == 1:
            ref = part(t, y + k, p)
            send(ref, ref, ll_s.at[t, k, p], ll_r.at[t, k, p], left)

    def a_start(t):
        send(a_st.at[t], a_full.at[t, y, zh], ac_s.at[t], ac_r.at[t], dev(1 - zh, x, c, zl, y))
        go(t, 0, 0)

    def a_cross(t):
        arrived(part(t, y, 1), ac_r.at[t])
        go(t, 0, 1)

    def a_ring(t, k):
        for p in (0, 1):
            arrived(part(t, y + 8 - k, p), rr_r.at[t, k - 1, p])
            arrived(part(t, y + k, p), ll_r.at[t, k - 1, p])
            go(t, k, p)

    def a_last(t):
        arrived(part(t, y + 4, 0), rr_r.at[t, 3, 0])
        arrived(part(t, y + 4, 1), ll_r.at[t, 3, 1])

    def owner(off, cc):
        base = held_rows((x + 4 - off) % 4, cc)
        return base, base // 256, (base // 128) % 2

    def project(t, off):
        for cc in range(2):
            base, zlt, hf = owner(off, cc)
            acc = jnp.zeros((128, TOK), F32)
            for yy in range(8):
                acc = acc + lax.dot_general(
                    wfull[pl.ds(base, 128), yy * 256:(yy + 1) * 256], a_full[t, yy].reshape(TOK, 256),
                    (((1,), (1,)), ((), ())), preferred_element_type=F32,
                )
            for zht in range(2):
                value = acc[:, zht * HALF:(zht + 1) * HALF].astype(BF)
                mine = (zht == zh) & (zlt == zl)

                @pl.when(mine)
                def _():
                    cin[t, z, hf] = value

                @pl.when(jnp.logical_not(mine))
                def _():
                    piece = cst.at[t, off, cc, zht]
                    piece[...] = value
                    send(piece, cin.at[t, z, hf], c_s.at[t, off, cc, zht], c_r.at[t, z, hf], dev(zht, x, c, zlt, y))

    def collect(t):
        for hf in range(2):
            total = cin[t, z, hf].astype(F32)
            for d in (1, 7, 2, 6, 3, 5, 4):
                zs = (z + d) % 8
                arrived(cin.at[t, zs, hf], c_r.at[t, zs, hf])
                total = total + cin[t, zs, hf].astype(F32)
            out_ref[hf * 128:(hf + 1) * 128, t * HALF:(t + 1) * HALF] = total.astype(BF)

    def kv_drain():
        @pl.when(zh == 0)
        def _():
            arrived(kv.at[s], kc_s)

        for off in (1, 2, 3):
            @pl.when(x + off < 4)
            def _():
                arrived(kv.at[s], kx_s.at[off])

            @pl.when(zh == 1)
            def _():
                arrived(kv.at[s], kxx_s.at[off])

        for xs in range(4):
            @pl.when(xs <= x)
            def _():
                arrived(kv.at[s], kd_s.at[zh * 4 + xs])

            @pl.when(zh == 1)
            def _():
                arrived(kv.at[s], kd_s.at[xs])

    def w_turn_drain():
        def w1_sent(n, carry):
            to = w1_place(n)

            @pl.when(jnp.logical_not((to[0] == s) & (to[1] == h)))
            def _():
                arrived(wst.at[n], w1_s.at[n])

            return carry

        lax.fori_loop(0, 32, w1_sent, 0)

    def w_pick_drain():
        arrived(whop, wh_s)
        for d in range(1, 8):
            arrived(w2s.at[d], w2_s.at[d])

    def w_gather_drain():
        for off in (1, 2, 3):
            for zq in range(8):
                arrived(wfull.at[row16(zq), :], wx_s.at[off, zq])
            arrived(chunk, wd_s.at[off])
        arrived(chunk, wd_s.at[0])

    def a_drain():
        for t in range(2):
            arrived(a_st.at[t], ac_s.at[t])
            for k in range(4):
                for p in (0, 1):
                    if k < 3 or p == 0:
                        arrived(part(t, y, 0), rr_s.at[t, k, p])
                    if k < 3 or p == 1:
                        arrived(part(t, y, 0), ll_s.at[t, k, p])

    def proj_drain():
        for t in range(2):
            for off in range(4):
                for cc in range(2):
                    zlt = owner(off, cc)[1]
                    for zht in range(2):
                        @pl.when(jnp.logical_not((zht == zh) & (zlt == zl)))
                        def _():
                            arrived(cst.at[t, off, cc, zht], c_s.at[t, off, cc, zht])

    entry()
    kv_first()
    all_in()
    kv_send()
    w_turn()
    w_hop()
    w_spread()
    kv_second()
    w_spread_far()
    kv_wait()
    attention(0)
    a_start(0)
    attention(1)
    a_start(1)
    a_cross(0)
    w_pick()
    a_ring(0, 1)
    a_cross(1)
    a_ring(0, 2)
    a_ring(1, 1)
    w_gather()
    a_ring(0, 3)
    a_ring(1, 2)
    a_last(0)
    w_share(1)
    w_share(3)
    w_shared(0)
    project(0, 0)
    a_ring(1, 3)
    w_shared(1)
    project(0, 1)
    w_shared(3)
    project(0, 3)
    a_last(1)
    project(1, 0)
    project(1, 1)
    project(1, 3)
    w_share(2)
    w_shared(2)
    project(0, 2)
    project(1, 2)
    collect(0)
    collect(1)
    kv_drain()
    w_turn_drain()
    w_pick_drain()
    w_gather_drain()
    a_drain()
    proj_drain()


def on_device(queries, key_rows, value_rows, value_turn, block_map, block_turn, out_weight):
    dma = pltpu.SemaphoreType.DMA
    return pl.pallas_call(
        kernel,
        out_shape=jax.ShapeDtypeStruct((256, TOK), BF),
        in_specs=[pl.BlockSpec(memory_space=pltpu.SMEM)] + [pl.BlockSpec(memory_space=pltpu.HBM)] * 6,
        out_specs=pl.BlockSpec(memory_space=pltpu.VMEM),
        scratch_shapes=[
            pltpu.VMEM((16, 2, TOK, HD), BF),
            pltpu.VMEM((2, 4, HALF, HD), BF),
            pltpu.VMEM((8, 4, HALF, 2 * TOK), F32),
            pltpu.VMEM((4, HALF, HD), F32),
            pltpu.VMEM((4, HALF, HD), F32),
            pltpu.VMEM((4, HALF, HD), F32),
            pltpu.VMEM((32, 4, 16, HD), BF),
            pltpu.VMEM((16, 4, 16, HD), BF),
            pltpu.VMEM((128, 16, HD), BF),
            pltpu.VMEM((8, 16, 2048), BF),
            pltpu.VMEM((1024, 2048), BF),
            pltpu.VMEM((2, HALF, 256), BF),
            pltpu.VMEM((2, 8, 2, HALF, 256), BF),
            pltpu.VMEM((2, 4, 2, 2, 128, HALF), BF),
            pltpu.VMEM((2, 8, 2, 128, HALF), BF),
            pltpu.VMEM((TOK, HD), BF),
            pltpu.VMEM((HD, HD), BF),
            pltpu.VMEM((512, 512), BF),
            pltpu.VMEM((4, HD, HD), BF),
            pltpu.VMEM((TOK, 512), BF),
            dma((6,)),
            dma(()), dma((4,)), dma((4,)), dma(()), dma((8,)), dma((8,)), dma((4,)), dma((4,)),
            dma(()), dma(()), dma((32,)), dma((32,)), dma((8,)), dma((8,)), dma((4, 8)), dma((4, 8)), dma((4,)), dma((4,)),
            dma((2,)), dma((2,)), dma((2, 4, 2)), dma((2, 4, 2)), dma((2, 4, 2)), dma((2, 4, 2)),
            dma((2, 4, 2, 2)), dma((2, 8, 2)),
        ],
        compiler_params=pltpu.CompilerParams(
            has_side_effects=True, collective_id=0, vmem_limit_bytes=60 * 1024 * 1024
        ),
    )(block_map, queries, key_rows, value_rows, value_turn, block_turn, out_weight)


def solution(mesh):
    placed = (
        P("seq", "head"),
        P("seq", None),
        P("seq", None),
        P(),
        P(),
        P("head", None, None),
        P("head", "seq"),
    )
    return jax.shard_map(
        on_device, mesh=mesh, in_specs=placed, out_specs=P("head", "seq"), check_vma=False
    )
```

```python
import math

import jax
import jax.numpy as jnp
from jax import lax
from jax.experimental import pallas as pl
from jax.experimental.pallas import tpu as pltpu
from jax.sharding import PartitionSpec as P

MESH = pl.DeviceIdType.MESH
BF = jnp.bfloat16
F32 = jnp.float32
HD = 128
TOK = 256
HALF = 128


def dev(zh, x, c, zl, y):
    return (zh * 8 + x * 2 + c, zl * 8 + y)


def send(src, dst, ssem, rsem, to):
    pltpu.make_async_remote_copy(
        src_ref=src, dst_ref=dst, send_sem=ssem, recv_sem=rsem, device_id=to, device_id_type=MESH
    ).start()


def arrived(slot, sem):
    pltpu.make_async_copy(slot, slot, sem).wait()


def kernel(
    map_ref, q_ref, key_ref, val_ref, vturn_ref, bturn_ref, w_ref, out_ref,
    kv, q_all, score, top_ref, total_ref, acc_ref, wst, whop, w1, w2s, wfull, a_st, a_full, cst, cin,
    val_in, vturn_in, w_in, bturn_in, q_in, in_s,
    kc_s, kx_s, kx_r, kc_r, kd_s, kd_r, kxx_s, kxx_r,
    wh_s, wh_r, w1_s, w1_r, w2_s, w2_r, wx_s, wx_r, wd_s, wd_r,
    ac_s, ac_r, rr_s, rr_r, ll_s, ll_r, c_s, c_r,
):
    s = lax.axis_index("seq")
    h = lax.axis_index("head")
    zh, x, c = s // 8, (s // 2) % 4, s % 2
    zl, y = h // 8, h % 8
    z = zh * 4 + zl

    g = zl * 2 + y // 4
    lanes = pl.ds(pl.multiple_of(g * HD, HD), HD)
    load_key = pltpu.make_async_copy(key_ref.at[:, lanes], kv.at[s, 0], in_s.at[0])
    load_val = pltpu.make_async_copy(val_ref.at[:, lanes], val_in, in_s.at[1])
    load_vturn = pltpu.make_async_copy(vturn_ref.at[g], vturn_in, in_s.at[2])
    load_w = pltpu.make_async_copy(w_ref, w_in, in_s.at[3])
    load_bturn = pltpu.make_async_copy(bturn_ref, bturn_in, in_s.at[4])
    load_q = pltpu.make_async_copy(q_ref, q_in, in_s.at[5])
    for load in (load_key, load_val, load_vturn, load_w, load_bturn, load_q):
        load.start()

    w_seq = zh * 8 + x * 2 + (y // 2) % 2
    w_at = zl * 2 + c

    def held_rows(xx, cc):
        hf = (xx + y // 4) % 2
        xs = (xx + 4 - hf) % 4
        return pl.multiple_of((2 * cc + xs // 2) * 256 + hf * 128, 128)

    rows = held_rows(x, c)

    def row16(base, m):
        return pl.ds(pl.multiple_of(base + m * 16, 16), 16)

    def w1_place(n):
        hf, r, m = n // 16, (n // 8) % 2, n % 8
        return dev(zh, x, m % 2, m // 2, 4 * ((x + hf) % 2) + 2 * c + r)

    chunk = wfull.at[pl.ds(rows, 128), :]
    right = dev(zh, x, c, zl, (y + 1) % 8)
    left = dev(zh, x, c, zl, (y + 7) % 8)

    barrier = pltpu.get_barrier_semaphore()

    def greet(to):
        pl.semaphore_signal(barrier, inc=1, device_id=to, device_id_type=MESH)

    def greet_w1(hh, carry):
        @pl.when(jnp.logical_not((w_seq == s) & (hh == h)))
        def _():
            greet((w_seq, hh))

        return carry

    def entry():
        for d in range(1, 8):
            zt = (z + d) % 8
            greet(dev(zt // 4, x, c, zt % 4, y))
        for off in (1, 2, 3):
            greet(dev(zh, (x + off) % 4, c, zl, y))
        greet(dev(zh, x, 1 - c, zl, y))
        greet(right)
        greet(left)
        lax.fori_loop(0, 32, greet_w1, 0)
        for m in range(8):
            @pl.when(jnp.logical_not((c == zh) & (m == w_at)))
            def _():
                greet(dev(c, x, m % 2, m // 2, y))


    def all_in():
        own = (w_seq == s).astype(jnp.int32) + (c == zh).astype(jnp.int32)
        pl.semaphore_wait(barrier, 53 - own)

    def kv_first():
        load_key.wait()
        load_val.wait()
        load_vturn.wait()
        kv[s, 1] = jnp.dot(val_in[...], vturn_in[...], preferred_element_type=F32).astype(BF)

    def kv_send():
        @pl.when(zh == 0)
        def _():
            send(kv.at[s], kv.at[s], kc_s, kc_r, dev(1, x, c, zl, y))

        for off in (1, 2, 3):
            @pl.when(x + off < 4)
            def _():
                send(kv.at[s], kv.at[s], kx_s.at[off], kx_r.at[x], dev(zh, x + off, c, zl, y))

        send(kv.at[s], kv.at[s], kd_s.at[zh * 4 + x], kd_r.at[zh * 4 + x], dev(zh, x, 1 - c, zl, y))

    def w_turn(hf):
        if hf == 1:
            load_w.wait()
            load_bturn.wait()
        for i in range(4):
            for r in range(2):
                turned = lax.dot_general(
                    w_in[i * HD:(i + 1) * HD, (2 * r + hf) * 128:(2 * r + hf + 1) * 128], bturn_in[i],
                    (((0,), (1,)), ((), ())), preferred_element_type=F32,
                ).astype(BF)
                wst[hf * 16 + r * 8:hf * 16 + r * 8 + 8, i] = turned.reshape(8, 16, HD)

    def w_hop():
        far = wst.at[pl.ds(16, 16)]
        send(far, whop, wh_s, wh_r, dev(zh, (x + 1) % 4, c, zl, y))

    def w1_send(n, src):
        to = w1_place(n)
        mine = (to[0] == s) & (to[1] == h)

        @pl.when(jnp.logical_not(mine))
        def _():
            send(src, w1.at[pl.ds(h * 4, 4)], w1_s.at[n], w1_r.at[h], to)

        @pl.when(mine)
        def _():
            pltpu.make_async_copy(src, w1.at[pl.ds(h * 4, 4)], w1_r.at[h]).start()

    def w_spread():
        def one(step, carry):
            n = (step + h) % 16
            w1_send(n, wst.at[n])
            return carry

        lax.fori_loop(0, 16, one, 0)

    def w_spread_far():
        arrived(whop, wh_r)

        def one(step, carry):
            n = (step + h) % 16
            w1_send(16 + n, whop.at[n])
            return carry

        lax.fori_loop(0, 16, one, 0)

    def kv_second():
        @pl.when(zh == 1)
        def _():
            arrived(kv.at[s - 8], kc_r)
            for off in (1, 3, 2):
                send(kv.at[s - 8], kv.at[s - 8], kxx_s.at[off], kxx_r.at[off], dev(1, (x + off) % 4, c, zl, y))
            send(kv.at[s - 8], kv.at[s - 8], kd_s.at[x], kd_r.at[x], dev(1, x, 1 - c, zl, y))

        for xs in range(3):
            @pl.when(xs < x)
            def _():
                slot = kv.at[zh * 8 + xs * 2 + c]
                arrived(slot, kx_r.at[xs])
                send(slot, slot, kd_s.at[zh * 4 + xs], kd_r.at[zh * 4 + xs], dev(zh, x, 1 - c, zl, y))

        @pl.when(zh == 1)
        def _():
            for off in (1, 3, 2):
                xs = (x + 4 - off) % 4
                slot = kv.at[xs * 2 + c]
                arrived(slot, kxx_r.at[off])
                send(slot, slot, kd_s.at[xs], kd_r.at[xs], dev(1, x, 1 - c, zl, y))

    def kv_wait():
        for xs in range(4):
            @pl.when(xs <= x)
            def _():
                arrived(kv.at[zh * 8 + xs * 2 + 1 - c], kd_r.at[zh * 4 + xs])

            @pl.when(zh == 1)
            def _():
                arrived(kv.at[xs * 2 + 1 - c], kd_r.at[xs])

    def w2_send(step, carry):
        zt = (z + step) % 8
        zht, zlt = zt // 4, zt % 4
        for kk in range(16):
            block = map_ref[(zlt * 8 + kk // 2) * 4 + zht * 2 + kk % 2]
            w2s[step, :, kk * HD:(kk + 1) * HD] = w1[block]

        there = wfull.at[row16(held_rows(x, zh), w_at), :]
        mine = (step == 0) & (c == zh)

        @pl.when(jnp.logical_not(mine))
        def _():
            send(w2s.at[step], there, w2_s.at[step], w2_r.at[w_at], dev(zht, x, zh, zlt, y))

        @pl.when(mine)
        def _():
            pltpu.make_async_copy(w2s.at[step], there, w2_r.at[w_at]).start()

        return carry

    def w_pick():
        for hh in range(32):
            arrived(w1.at[pl.ds(hh * 4, 4)], w1_r.at[hh])
        lax.fori_loop(0, 8, w2_send, 0)

    def w_gather():
        for m in range(8):
            piece = wfull.at[row16(rows, m), :]
            arrived(piece, w2_r.at[m])
            for off in (1, 3):
                send(piece, piece, wx_s.at[off, m], wx_r.at[off, m], dev(zh, (x + off) % 4, c, zl, y))
        send(chunk, chunk, wd_s.at[0], wd_r.at[0], dev(zh, x, 1 - c, zl, y))

    def w_share(off):
        base = held_rows((x + 4 - off) % 4, c)
        for zq in range(8):
            piece = wfull.at[pl.ds(pl.multiple_of(base + zq * 16, 16), 16), :]
            arrived(piece, wx_r.at[off, zq])
            if off == 1 and zq < 4 or off == 3 and zq >= 4:
                onward = dev(zh, (x + off) % 4, c, zl, y)
                send(piece, piece, wx_s.at[2, zq], wx_r.at[2, zq], onward)
        theirs = wfull.at[pl.ds(base, 128), :]
        send(theirs, theirs, wd_s.at[off], wd_r.at[off], dev(zh, x, 1 - c, zl, y))

    def w_shared(off):
        base = held_rows((x + 4 - off) % 4, 1 - c)
        arrived(wfull.at[pl.ds(base, 128), :], wd_r.at[off])

    turn = math.log2(math.e) / math.sqrt(HD)
    last = zh * 4 + x

    def attention(t):
        def scored(i, u, j):
            return lax.dot_general(
                q_all[t, i], kv[2 * u + j, 0], (((1,), (1,)), ((), ())), preferred_element_type=F32
            )

        if t == 0:
            load_q.wait()
        for i in range(4):
            q_all[t, i] = q_in[t * HALF:(t + 1) * HALF, i * HD:(i + 1) * HD]
        place = lax.broadcasted_iota(jnp.int32, (HALF, TOK), 0) + (c * TOK + t * HALF)
        key_at = lax.broadcasted_iota(jnp.int32, (HALF, TOK), 1)
        for i in range(4):
            top = None
            for j in range(2):
                value = jnp.where(key_at + j * TOK <= place, scored(i, last, j), F32(-1e30))
                score[last, i, :, j * TOK:(j + 1) * TOK] = value
                value = jnp.maximum(value[:, :HD], value[:, HD:])
                top = value if top is None else jnp.maximum(top, value)
            top_ref[i] = top

        def first(u, carry):
            for i in range(4):
                top = top_ref[i]
                for j in range(2):
                    value = scored(i, u, j)
                    score[u, i, :, j * TOK:(j + 1) * TOK] = value
                    top = jnp.maximum(top, jnp.maximum(value[:, :HD], value[:, HD:]))
                top_ref[i] = top
            return carry

        lax.fori_loop(0, last, first, 0)
        for i in range(4):
            top_ref[i] = jnp.broadcast_to(jnp.max(top_ref[i], axis=1, keepdims=True) * turn, (HALF, HD))
        total_ref[...] = jnp.zeros_like(total_ref)
        acc_ref[...] = jnp.zeros_like(acc_ref)

        def second(u, carry):
            for i in range(4):
                top = top_ref[i]
                total = total_ref[i]
                acc = acc_ref[i]
                for j in range(2):
                    weight = []
                    for k in range(2):
                        lane = j * TOK + k * HD
                        weight.append(jnp.exp2(score[u, i, :, lane:lane + HD] * turn - top))
                        total = total + weight[k]
                    acc = acc + jnp.dot(
                        jnp.concatenate(weight, axis=1).astype(BF), kv[2 * u + j, 1], preferred_element_type=F32
                    )
                total_ref[i] = total
                acc_ref[i] = acc
            return carry

        lax.fori_loop(0, last + 1, second, 0)

        def head(i):
            return (acc_ref[i] / jnp.sum(total_ref[i], axis=1, keepdims=True)).astype(BF)

        for k in range(2):
            @pl.when(zh == k)
            def _():
                for i in range(2):
                    a_full[t, y, zh, :, i * HD:(i + 1) * HD] = head(2 * k + i)
                    a_st[t, :, i * HD:(i + 1) * HD] = head(2 * (1 - k) + i)

    def part(t, slot, p):
        return a_full.at[t, slot % 8, zh if p == 0 else 1 - zh]

    def go(t, k, p):
        if k < 3 or p == 0:
            ref = part(t, y + 8 - k, p)
            send(ref, ref, rr_s.at[t, k, p], rr_r.at[t, k, p], right)
        if k < 3 or p == 1:
            ref = part(t, y + k, p)
            send(ref, ref, ll_s.at[t, k, p], ll_r.at[t, k, p], left)

    def a_start(t):
        send(a_st.at[t], a_full.at[t, y, zh], ac_s.at[t], ac_r.at[t], dev(1 - zh, x, c, zl, y))
        go(t, 0, 0)

    def a_cross(t):
        arrived(part(t, y, 1), ac_r.at[t])
        go(t, 0, 1)

    def a_ring(t, k):
        for p in (0, 1):
            arrived(part(t, y + 8 - k, p), rr_r.at[t, k - 1, p])
            arrived(part(t, y + k, p), ll_r.at[t, k - 1, p])
            go(t, k, p)

    def a_last(t):
        arrived(part(t, y + 4, 0), rr_r.at[t, 3, 0])
        arrived(part(t, y + 4, 1), ll_r.at[t, 3, 1])

    def owner(off, cc):
        base = held_rows((x + 4 - off) % 4, cc)
        return base, base // 256, (base // 128) % 2

    def project(t, off):
        for cc in range(2):
            base, zlt, hf = owner(off, cc)
            acc = jnp.zeros((128, TOK), F32)
            for yy in range(8):
                acc = acc + lax.dot_general(
                    wfull[pl.ds(base, 128), yy * 256:(yy + 1) * 256], a_full[t, yy].reshape(TOK, 256),
                    (((1,), (1,)), ((), ())), preferred_element_type=F32,
                )
            for zht in range(2):
                value = acc[:, zht * HALF:(zht + 1) * HALF].astype(BF)
                mine = (zht == zh) & (zlt == zl)

                @pl.when(mine)
                def _():
                    cin[t, z, hf] = value

                @pl.when(jnp.logical_not(mine))
                def _():
                    piece = cst.at[t, off, cc, zht]
                    piece[...] = value
                    send(piece, cin.at[t, z, hf], c_s.at[t, off, cc, zht], c_r.at[t, z, hf], dev(zht, x, c, zlt, y))

    def collect(t):
        for hf in range(2):
            total = cin[t, z, hf].astype(F32)
            for d in (1, 7, 2, 6, 3, 5, 4):
                zs = (z + d) % 8
                arrived(cin.at[t, zs, hf], c_r.at[t, zs, hf])
                total = total + cin[t, zs, hf].astype(F32)
            out_ref[hf * 128:(hf + 1) * 128, t * HALF:(t + 1) * HALF] = total.astype(BF)

    def kv_drain():
        @pl.when(zh == 0)
        def _():
            arrived(kv.at[s], kc_s)

        for off in (1, 2, 3):
            @pl.when(x + off < 4)
            def _():
                arrived(kv.at[s], kx_s.at[off])

            @pl.when(zh == 1)
            def _():
                arrived(kv.at[s], kxx_s.at[off])

        for xs in range(4):
            @pl.when(xs <= x)
            def _():
                arrived(kv.at[s], kd_s.at[zh * 4 + xs])

            @pl.when(zh == 1)
            def _():
                arrived(kv.at[s], kd_s.at[xs])

    def w_turn_drain():
        def w1_sent(n, carry):
            to = w1_place(n)

            @pl.when(jnp.logical_not((to[0] == s) & (to[1] == h)))
            def _():
                arrived(wst.at[n], w1_s.at[n])

            return carry

        lax.fori_loop(0, 32, w1_sent, 0)

    def w_pick_drain():
        arrived(whop, wh_s)
        for d in range(1, 8):
            arrived(w2s.at[d], w2_s.at[d])

        @pl.when(c != zh)
        def _():
            arrived(w2s.at[0], w2_s.at[0])


    def w_gather_drain():
        for off in (1, 2, 3):
            for zq in range(8):
                arrived(wfull.at[row16(rows, zq), :], wx_s.at[off, zq])
            arrived(chunk, wd_s.at[off])
        arrived(chunk, wd_s.at[0])

    def a_drain():
        for t in range(2):
            arrived(a_st.at[t], ac_s.at[t])
            for k in range(4):
                for p in (0, 1):
                    if k < 3 or p == 0:
                        arrived(part(t, y, 0), rr_s.at[t, k, p])
                    if k < 3 or p == 1:
                        arrived(part(t, y, 0), ll_s.at[t, k, p])

    def proj_drain():
        for t in range(2):
            for off in range(4):
                for cc in range(2):
                    zlt = owner(off, cc)[1]
                    for zht in range(2):
                        @pl.when(jnp.logical_not((zht == zh) & (zlt == zl)))
                        def _():
                            arrived(cst.at[t, off, cc, zht], c_s.at[t, off, cc, zht])

    entry()
    kv_first()
    all_in()
    kv_send()
    w_turn(1)
    w_hop()
    w_turn(0)
    kv_second()
    w_spread()
    w_spread_far()
    kv_wait()
    attention(0)
    a_start(0)
    attention(1)
    a_start(1)
    a_cross(0)
    w_pick()
    a_ring(0, 1)
    a_cross(1)
    a_ring(0, 2)
    a_ring(1, 1)
    w_gather()
    a_ring(0, 3)
    a_ring(1, 2)
    a_last(0)
    w_share(1)
    w_share(3)
    w_shared(0)
    project(0, 0)
    a_ring(1, 3)
    w_shared(1)
    project(0, 1)
    w_shared(3)
    project(0, 3)
    a_last(1)
    project(1, 0)
    project(1, 1)
    project(1, 3)
    w_share(2)
    w_shared(2)
    project(0, 2)
    project(1, 2)
    kv_drain()
    w_turn_drain()
    w_pick_drain()
    w_gather_drain()
    a_drain()
    collect(0)
    collect(1)
    proj_drain()


def on_device(queries, key_rows, value_rows, value_turn, block_map, block_turn, out_weight):
    dma = pltpu.SemaphoreType.DMA
    return pl.pallas_call(
        kernel,
        out_shape=jax.ShapeDtypeStruct((256, TOK), BF),
        in_specs=[pl.BlockSpec(memory_space=pltpu.SMEM)] + [pl.BlockSpec(memory_space=pltpu.HBM)] * 6,
        out_specs=pl.BlockSpec(memory_space=pltpu.VMEM),
        scratch_shapes=[
            pltpu.VMEM((16, 2, TOK, HD), BF),
            pltpu.VMEM((2, 4, HALF, HD), BF),
            pltpu.VMEM((8, 4, HALF, 2 * TOK), F32),
            pltpu.VMEM((4, HALF, HD), F32),
            pltpu.VMEM((4, HALF, HD), F32),
            pltpu.VMEM((4, HALF, HD), F32),
            pltpu.VMEM((32, 4, 16, HD), BF),
            pltpu.VMEM((16, 4, 16, HD), BF),
            pltpu.VMEM((128, 16, HD), BF),
            pltpu.VMEM((8, 16, 2048), BF),
            pltpu.VMEM((1024, 2048), BF),
            pltpu.VMEM((2, HALF, 256), BF),
            pltpu.VMEM((2, 8, 2, HALF, 256), BF),
            pltpu.VMEM((2, 4, 2, 2, 128, HALF), BF),
            pltpu.VMEM((2, 8, 2, 128, HALF), BF),
            pltpu.VMEM((TOK, HD), BF),
            pltpu.VMEM((HD, HD), BF),
            pltpu.VMEM((512, 512), BF),
            pltpu.VMEM((4, HD, HD), BF),
            pltpu.VMEM((TOK, 512), BF),
            dma((6,)),
            dma(()), dma((4,)), dma((4,)), dma(()), dma((8,)), dma((8,)), dma((4,)), dma((4,)),
            dma(()), dma(()), dma((32,)), dma((32,)), dma((8,)), dma((8,)), dma((4, 8)), dma((4, 8)), dma((4,)), dma((4,)),
            dma((2,)), dma((2,)), dma((2, 4, 2)), dma((2, 4, 2)), dma((2, 4, 2)), dma((2, 4, 2)),
            dma((2, 4, 2, 2)), dma((2, 8, 2)),
        ],
        compiler_params=pltpu.CompilerParams(
            has_side_effects=True, collective_id=0, vmem_limit_bytes=60 * 1024 * 1024
        ),
    )(block_map, queries, key_rows, value_rows, value_turn, block_turn, out_weight)


def solution(mesh):
    placed = (
        P("seq", "head"),
        P("seq", None),
        P("seq", None),
        P(),
        P(),
        P("head", None, None),
        P("head", "seq"),
    )
    return jax.shard_map(
        on_device, mesh=mesh, in_specs=placed, out_specs=P("head", "seq"), check_vma=False
    )
```

```python
import math

import jax
import jax.numpy as jnp
from jax import lax
from jax.experimental import pallas as pl
from jax.experimental.pallas import tpu as pltpu
from jax.sharding import PartitionSpec as P

MESH = pl.DeviceIdType.MESH
BF = jnp.bfloat16
F32 = jnp.float32
HD = 128
TOK = 256
HALF = 128


def dev(zh, x, c, zl, y):
    return (zh * 8 + x * 2 + c, zl * 8 + y)


def send(src, dst, ssem, rsem, to):
    pltpu.make_async_remote_copy(
        src_ref=src, dst_ref=dst, send_sem=ssem, recv_sem=rsem, device_id=to, device_id_type=MESH
    ).start()


def arrived(slot, sem):
    pltpu.make_async_copy(slot, slot, sem).wait()


def kernel(
    map_ref, q_ref, key_ref, val_ref, vturn_ref, bturn_ref, w_ref, out_ref,
    kv, q_all, score, top_ref, total_ref, acc_ref, wst, whop, w1, w2s, wfull, a_st, a_full, cst, cin,
    val_in, vturn_in, w_in, bturn_in, q_in, in_s,
    kc_s, kx_s, kx_r, kc_r, kd_s, kd_r, kxx_s, kxx_r,
    wh_s, wh_r, w1_s, w1_r, w2_s, w2_r, wx_s, wx_r, wd_s, wd_r,
    ac_s, ac_r, rr_s, rr_r, ll_s, ll_r, c_s, c_r,
):
    s = lax.axis_index("seq")
    h = lax.axis_index("head")
    zh, x, c = s // 8, (s // 2) % 4, s % 2
    zl, y = h // 8, h % 8
    z = zh * 4 + zl

    g = zl * 2 + y // 4
    lanes = pl.ds(pl.multiple_of(g * HD, HD), HD)
    load_key = pltpu.make_async_copy(key_ref.at[:, lanes], kv.at[s, 0], in_s.at[0])
    load_val = pltpu.make_async_copy(val_ref.at[:, lanes], val_in, in_s.at[1])
    load_vturn = pltpu.make_async_copy(vturn_ref.at[g], vturn_in, in_s.at[2])
    load_w = pltpu.make_async_copy(w_ref, w_in, in_s.at[3])
    load_bturn = pltpu.make_async_copy(bturn_ref, bturn_in, in_s.at[4])
    load_q = pltpu.make_async_copy(q_ref, q_in, in_s.at[5])
    for load in (load_key, load_val, load_vturn, load_w, load_bturn, load_q):
        load.start()

    w_seq = zh * 8 + x * 2 + (y // 2) % 2
    w_at = zl * 2 + c

    def held_rows(xx, cc):
        hf = (xx + y // 4) % 2
        xs = (xx + 4 - hf) % 4
        return pl.multiple_of((2 * cc + xs // 2) * 256 + hf * 128, 128)

    rows = held_rows(x, c)

    def lanes1024(k):
        return pl.ds(pl.multiple_of(k * 1024, 1024), 1024)

    def row16(base, m):
        return pl.ds(pl.multiple_of(base + m * 16, 16), 16)

    def w1_place(n):
        hf, r, m = n // 16, (n // 8) % 2, n % 8
        return dev(zh, x, m % 2, m // 2, 4 * ((x + hf) % 2) + 2 * c + r)

    chunk = wfull.at[pl.ds(rows, 128), :]
    right = dev(zh, x, c, zl, (y + 1) % 8)
    left = dev(zh, x, c, zl, (y + 7) % 8)

    barrier = pltpu.get_barrier_semaphore()

    def greet(to):
        pl.semaphore_signal(barrier, inc=1, device_id=to, device_id_type=MESH)

    def greet_w1(hh, carry):
        @pl.when(jnp.logical_not((w_seq == s) & (hh == h)))
        def _():
            greet((w_seq, hh))

        return carry

    def entry():
        for d in range(1, 8):
            zt = (z + d) % 8
            greet(dev(zt // 4, x, c, zt % 4, y))
        for off in (1, 2, 3):
            greet(dev(zh, (x + off) % 4, c, zl, y))
        greet(dev(zh, x, 1 - c, zl, y))
        greet(right)
        greet(left)
        lax.fori_loop(0, 32, greet_w1, 0)
        for m in range(8):
            @pl.when(jnp.logical_not((c == zh) & (m == w_at)))
            def _():
                greet(dev(c, x, m % 2, m // 2, y))


    def all_in():
        own = (w_seq == s).astype(jnp.int32) + (c == zh).astype(jnp.int32)
        pl.semaphore_wait(barrier, 53 - own)

    def kv_first():
        load_key.wait()
        load_val.wait()
        load_vturn.wait()
        kv[s, 1] = jnp.dot(val_in[...], vturn_in[...], preferred_element_type=F32).astype(BF)

    def kv_send():
        @pl.when(zh == 0)
        def _():
            send(kv.at[s], kv.at[s], kc_s, kc_r, dev(1, x, c, zl, y))

        for off in (1, 2, 3):
            @pl.when(x + off < 4)
            def _():
                send(kv.at[s], kv.at[s], kx_s.at[off], kx_r.at[x], dev(zh, x + off, c, zl, y))

        send(kv.at[s], kv.at[s], kd_s.at[zh * 4 + x], kd_r.at[zh * 4 + x], dev(zh, x, 1 - c, zl, y))

    def w_turn(hf):
        if hf == 1:
            load_w.wait()
            load_bturn.wait()
        for i in range(4):
            for r in range(2):
                turned = lax.dot_general(
                    w_in[i * HD:(i + 1) * HD, (2 * r + hf) * 128:(2 * r + hf + 1) * 128], bturn_in[i],
                    (((0,), (1,)), ((), ())), preferred_element_type=F32,
                ).astype(BF)
                wst[hf * 16 + r * 8:hf * 16 + r * 8 + 8, i] = turned.reshape(8, 16, HD)

    def w_hop():
        far = wst.at[pl.ds(16, 16)]
        send(far, whop, wh_s, wh_r, dev(zh, (x + 1) % 4, c, zl, y))

    def w1_send(n, src):
        to = w1_place(n)
        mine = (to[0] == s) & (to[1] == h)

        @pl.when(jnp.logical_not(mine))
        def _():
            send(src, w1.at[pl.ds(h * 4, 4)], w1_s.at[n], w1_r.at[h], to)

        @pl.when(mine)
        def _():
            pltpu.make_async_copy(src, w1.at[pl.ds(h * 4, 4)], w1_r.at[h]).start()

    def w_spread():
        def one(step, carry):
            n = (step + h) % 16
            w1_send(n, wst.at[n])
            return carry

        lax.fori_loop(0, 16, one, 0)

    def w_spread_far():
        arrived(whop, wh_r)

        def one(step, carry):
            n = (step + h) % 16
            w1_send(16 + n, whop.at[n])
            return carry

        lax.fori_loop(0, 16, one, 0)

    def kv_second():
        @pl.when(zh == 1)
        def _():
            arrived(kv.at[s - 8], kc_r)
            for off in (1, 3, 2):
                send(kv.at[s - 8], kv.at[s - 8], kxx_s.at[off], kxx_r.at[off], dev(1, (x + off) % 4, c, zl, y))
            send(kv.at[s - 8], kv.at[s - 8], kd_s.at[x], kd_r.at[x], dev(1, x, 1 - c, zl, y))

        for xs in range(3):
            @pl.when(xs < x)
            def _():
                slot = kv.at[zh * 8 + xs * 2 + c]
                arrived(slot, kx_r.at[xs])
                send(slot, slot, kd_s.at[zh * 4 + xs], kd_r.at[zh * 4 + xs], dev(zh, x, 1 - c, zl, y))

        @pl.when(zh == 1)
        def _():
            for off in (1, 3, 2):
                xs = (x + 4 - off) % 4
                slot = kv.at[xs * 2 + c]
                arrived(slot, kxx_r.at[off])
                send(slot, slot, kd_s.at[xs], kd_r.at[xs], dev(1, x, 1 - c, zl, y))

    def kv_wait():
        for xs in range(4):
            @pl.when(xs <= x)
            def _():
                arrived(kv.at[zh * 8 + xs * 2 + 1 - c], kd_r.at[zh * 4 + xs])

            @pl.when(zh == 1)
            def _():
                arrived(kv.at[xs * 2 + 1 - c], kd_r.at[xs])

    def w2_send(n, carry):
        k, step = n // 8, n % 8
        zt = (z + step) % 8
        zht, zlt = zt // 4, zt % 4
        for kk in range(8):
            block = map_ref[(zlt * 8 + k * 4 + kk // 2) * 4 + zht * 2 + kk % 2]
            w2s[k, step, :, kk * HD:(kk + 1) * HD] = w1[block]
        src = w2s.at[k, step]
        there = wfull.at[row16(held_rows(x, zh), w_at), lanes1024(k)]
        mine = (step == 0) & (c == zh)

        @pl.when(jnp.logical_not(mine))
        def _():
            send(src, there, w2_s.at[k, step], w2_r.at[k, w_at], dev(zht, x, zh, zlt, y))

        @pl.when(mine)
        def _():
            pltpu.make_async_copy(src, there, w2_r.at[k, w_at]).start()

        return carry

    def w_pick():
        for hh in range(32):
            arrived(w1.at[pl.ds(hh * 4, 4)], w1_r.at[hh])
        lax.fori_loop(0, 16, w2_send, 0)

    def w_gather(k):
        for m in range(8):
            piece = wfull.at[row16(rows, m), lanes1024(k)]
            arrived(piece, w2_r.at[k, m])
            for off in (1, 3):
                send(piece, piece, wx_s.at[off, k, m], wx_r.at[off, k, m], dev(zh, (x + off) % 4, c, zl, y))
        if k == 1:
            send(chunk, chunk, wd_s.at[0], wd_r.at[0], dev(zh, x, 1 - c, zl, y))

    def w_relay(off, k):
        base = held_rows((x + 4 - off) % 4, c)
        for m in range(8):
            piece = wfull.at[row16(base, m), lanes1024(k)]
            arrived(piece, wx_r.at[off, k, m])
            if off == 1 and m < 4 or off == 3 and m >= 4:
                send(piece, piece, wx_s.at[2, k, m], wx_r.at[2, k, m], dev(zh, (x + off) % 4, c, zl, y))
        if k == 1:
            theirs = wfull.at[pl.ds(base, 128), :]
            send(theirs, theirs, wd_s.at[off], wd_r.at[off], dev(zh, x, 1 - c, zl, y))

    def w_shared(off):
        base = held_rows((x + 4 - off) % 4, 1 - c)
        arrived(wfull.at[pl.ds(base, 128), :], wd_r.at[off])

    turn = math.log2(math.e) / math.sqrt(HD)
    last = zh * 4 + x

    def attention(t):
        def scored(i, u, j):
            return lax.dot_general(
                q_all[t, i], kv[2 * u + j, 0], (((1,), (1,)), ((), ())), preferred_element_type=F32
            )

        if t == 0:
            load_q.wait()
        for i in range(4):
            q_all[t, i] = q_in[t * HALF:(t + 1) * HALF, i * HD:(i + 1) * HD]
        place = lax.broadcasted_iota(jnp.int32, (HALF, TOK), 0) + (c * TOK + t * HALF)
        key_at = lax.broadcasted_iota(jnp.int32, (HALF, TOK), 1)
        for i in range(4):
            top = None
            for j in range(2):
                value = jnp.where(key_at + j * TOK <= place, scored(i, last, j), F32(-1e30))
                score[last, i, :, j * TOK:(j + 1) * TOK] = value
                value = jnp.maximum(value[:, :HD], value[:, HD:])
                top = value if top is None else jnp.maximum(top, value)
            top_ref[i] = top

        def first(u, carry):
            for i in range(4):
                top = top_ref[i]
                for j in range(2):
                    value = scored(i, u, j)
                    score[u, i, :, j * TOK:(j + 1) * TOK] = value
                    top = jnp.maximum(top, jnp.maximum(value[:, :HD], value[:, HD:]))
                top_ref[i] = top
            return carry

        lax.fori_loop(0, last, first, 0)
        for i in range(4):
            top_ref[i] = jnp.broadcast_to(jnp.max(top_ref[i], axis=1, keepdims=True) * turn, (HALF, HD))
        total_ref[...] = jnp.zeros_like(total_ref)
        acc_ref[...] = jnp.zeros_like(acc_ref)

        def second(u, carry):
            for i in range(4):
                top = top_ref[i]
                total = total_ref[i]
                acc = acc_ref[i]
                for j in range(2):
                    weight = []
                    for k in range(2):
                        lane = j * TOK + k * HD
                        weight.append(jnp.exp2(score[u, i, :, lane:lane + HD] * turn - top))
                        total = total + weight[k]
                    acc = acc + jnp.dot(
                        jnp.concatenate(weight, axis=1).astype(BF), kv[2 * u + j, 1], preferred_element_type=F32
                    )
                total_ref[i] = total
                acc_ref[i] = acc
            return carry

        lax.fori_loop(0, last + 1, second, 0)

        def head(i):
            return (acc_ref[i] / jnp.sum(total_ref[i], axis=1, keepdims=True)).astype(BF)

        for k in range(2):
            @pl.when(zh == k)
            def _():
                for i in range(2):
                    a_full[t, y, zh, :, i * HD:(i + 1) * HD] = head(2 * k + i)
                    a_st[t, :, i * HD:(i + 1) * HD] = head(2 * (1 - k) + i)

    def part(t, slot, p):
        return a_full.at[t, slot % 8, zh if p == 0 else 1 - zh]

    def go(t, k, p):
        if k < 3 or p == 0:
            ref = part(t, y + 8 - k, p)
            send(ref, ref, rr_s.at[t, k, p], rr_r.at[t, k, p], right)
        if k < 3 or p == 1:
            ref = part(t, y + k, p)
            send(ref, ref, ll_s.at[t, k, p], ll_r.at[t, k, p], left)

    def a_start(t):
        send(a_st.at[t], a_full.at[t, y, zh], ac_s.at[t], ac_r.at[t], dev(1 - zh, x, c, zl, y))
        go(t, 0, 0)

    def a_cross(t):
        arrived(part(t, y, 1), ac_r.at[t])
        go(t, 0, 1)

    def a_ring(t, k):
        for p in (0, 1):
            arrived(part(t, y + 8 - k, p), rr_r.at[t, k - 1, p])
            arrived(part(t, y + k, p), ll_r.at[t, k - 1, p])
            go(t, k, p)

    def a_last(t):
        arrived(part(t, y + 4, 0), rr_r.at[t, 3, 0])
        arrived(part(t, y + 4, 1), ll_r.at[t, 3, 1])

    def owner(off, cc):
        base = held_rows((x + 4 - off) % 4, cc)
        return base, base // 256, (base // 128) % 2

    def project(t, off):
        for cc in range(2):
            base, zlt, hf = owner(off, cc)
            acc = jnp.zeros((128, TOK), F32)
            for yy in range(8):
                acc = acc + lax.dot_general(
                    wfull[pl.ds(base, 128), yy * 256:(yy + 1) * 256], a_full[t, yy].reshape(TOK, 256),
                    (((1,), (1,)), ((), ())), preferred_element_type=F32,
                )
            for zht in range(2):
                value = acc[:, zht * HALF:(zht + 1) * HALF].astype(BF)
                mine = (zht == zh) & (zlt == zl)

                @pl.when(mine)
                def _():
                    cin[t, z, hf] = value

                @pl.when(jnp.logical_not(mine))
                def _():
                    piece = cst.at[t, off, cc, zht]
                    piece[...] = value
                    send(piece, cin.at[t, z, hf], c_s.at[t, off, cc, zht], c_r.at[t, z, hf], dev(zht, x, c, zlt, y))

    def collect(t):
        for hf in range(2):
            total = cin[t, z, hf].astype(F32)
            for d in (1, 7, 2, 6, 3, 5, 4):
                zs = (z + d) % 8
                arrived(cin.at[t, zs, hf], c_r.at[t, zs, hf])
                total = total + cin[t, zs, hf].astype(F32)
            out_ref[hf * 128:(hf + 1) * 128, t * HALF:(t + 1) * HALF] = total.astype(BF)

    def kv_drain():
        @pl.when(zh == 0)
        def _():
            arrived(kv.at[s], kc_s)

        for off in (1, 2, 3):
            @pl.when(x + off < 4)
            def _():
                arrived(kv.at[s], kx_s.at[off])

            @pl.when(zh == 1)
            def _():
                arrived(kv.at[s], kxx_s.at[off])

        for xs in range(4):
            @pl.when(xs <= x)
            def _():
                arrived(kv.at[s], kd_s.at[zh * 4 + xs])

            @pl.when(zh == 1)
            def _():
                arrived(kv.at[s], kd_s.at[xs])

    def w_turn_drain():
        def w1_sent(n, carry):
            to = w1_place(n)

            @pl.when(jnp.logical_not((to[0] == s) & (to[1] == h)))
            def _():
                arrived(wst.at[n], w1_s.at[n])

            return carry

        lax.fori_loop(0, 32, w1_sent, 0)

    def w_pick_drain():
        arrived(whop, wh_s)
        for k in range(2):
            for d in range(1, 8):
                arrived(w2s.at[k, d], w2_s.at[k, d])

            @pl.when(c != zh)
            def _():
                arrived(w2s.at[k, 0], w2_s.at[k, 0])

    def w_gather_drain():
        for off in (1, 2, 3):
            for k in range(2):
                for m in range(8):
                    arrived(wfull.at[row16(rows, m), lanes1024(k)], wx_s.at[off, k, m])
            arrived(chunk, wd_s.at[off])
        arrived(chunk, wd_s.at[0])

    def a_drain():
        for t in range(2):
            arrived(a_st.at[t], ac_s.at[t])
            for k in range(4):
                for p in (0, 1):
                    if k < 3 or p == 0:
                        arrived(part(t, y, 0), rr_s.at[t, k, p])
                    if k < 3 or p == 1:
                        arrived(part(t, y, 0), ll_s.at[t, k, p])

    def proj_drain():
        for t in range(2):
            for off in range(4):
                for cc in range(2):
                    zlt = owner(off, cc)[1]
                    for zht in range(2):
                        @pl.when(jnp.logical_not((zht == zh) & (zlt == zl)))
                        def _():
                            arrived(cst.at[t, off, cc, zht], c_s.at[t, off, cc, zht])

    entry()
    kv_first()
    all_in()
    kv_send()
    w_turn(1)
    w_hop()
    w_turn(0)
    kv_second()
    w_spread()
    w_spread_far()
    kv_wait()
    attention(0)
    a_start(0)
    attention(1)
    a_start(1)
    a_cross(0)
    w_pick()
    a_ring(0, 1)
    a_cross(1)
    a_ring(0, 2)
    w_gather(0)
    a_ring(1, 1)
    w_gather(1)
    a_ring(0, 3)
    w_relay(1, 0)
    w_relay(3, 0)
    a_ring(1, 2)
    a_last(0)
    w_shared(0)
    project(0, 0)
    w_relay(1, 1)
    w_relay(3, 1)
    a_ring(1, 3)
    w_shared(1)
    project(0, 1)
    w_shared(3)
    project(0, 3)
    a_last(1)
    project(1, 0)
    project(1, 1)
    project(1, 3)
    w_relay(2, 0)
    w_relay(2, 1)
    w_shared(2)
    project(0, 2)
    project(1, 2)
    kv_drain()
    w_turn_drain()
    w_pick_drain()
    w_gather_drain()
    a_drain()
    collect(0)
    collect(1)
    proj_drain()


def on_device(queries, key_rows, value_rows, value_turn, block_map, block_turn, out_weight):
    dma = pltpu.SemaphoreType.DMA
    return pl.pallas_call(
        kernel,
        out_shape=jax.ShapeDtypeStruct((256, TOK), BF),
        in_specs=[pl.BlockSpec(memory_space=pltpu.SMEM)] + [pl.BlockSpec(memory_space=pltpu.HBM)] * 6,
        out_specs=pl.BlockSpec(memory_space=pltpu.VMEM),
        scratch_shapes=[
            pltpu.VMEM((16, 2, TOK, HD), BF),
            pltpu.VMEM((2, 4, HALF, HD), BF),
            pltpu.VMEM((8, 4, HALF, 2 * TOK), F32),
            pltpu.VMEM((4, HALF, HD), F32),
            pltpu.VMEM((4, HALF, HD), F32),
            pltpu.VMEM((4, HALF, HD), F32),
            pltpu.VMEM((32, 4, 16, HD), BF),
            pltpu.VMEM((16, 4, 16, HD), BF),
            pltpu.VMEM((128, 16, HD), BF),
            pltpu.VMEM((2, 8, 16, 1024), BF),
            pltpu.VMEM((1024, 2048), BF),
            pltpu.VMEM((2, HALF, 256), BF),
            pltpu.VMEM((2, 8, 2, HALF, 256), BF),
            pltpu.VMEM((2, 4, 2, 2, 128, HALF), BF),
            pltpu.VMEM((2, 8, 2, 128, HALF), BF),
            pltpu.VMEM((TOK, HD), BF),
            pltpu.VMEM((HD, HD), BF),
            pltpu.VMEM((512, 512), BF),
            pltpu.VMEM((4, HD, HD), BF),
            pltpu.VMEM((TOK, 512), BF),
            dma((6,)),
            dma(()), dma((4,)), dma((4,)), dma(()), dma((8,)), dma((8,)), dma((4,)), dma((4,)),
            dma(()), dma(()), dma((32,)), dma((32,)), dma((2, 8)), dma((2, 8)), dma((4, 2, 8)), dma((4, 2, 8)), dma((4,)), dma((4,)),
            dma((2,)), dma((2,)), dma((2, 4, 2)), dma((2, 4, 2)), dma((2, 4, 2)), dma((2, 4, 2)),
            dma((2, 4, 2, 2)), dma((2, 8, 2)),
        ],
        compiler_params=pltpu.CompilerParams(
            has_side_effects=True, collective_id=0, vmem_limit_bytes=60 * 1024 * 1024
        ),
    )(block_map, queries, key_rows, value_rows, value_turn, block_turn, out_weight)


def solution(mesh):
    placed = (
        P("seq", "head"),
        P("seq", None),
        P("seq", None),
        P(),
        P(),
        P("head", None, None),
        P("head", "seq"),
    )
    return jax.shard_map(
        on_device, mesh=mesh, in_specs=placed, out_specs=P("head", "seq"), check_vma=False
    )
```

```python
import math

import jax
import jax.numpy as jnp
from jax import lax
from jax.experimental import pallas as pl
from jax.experimental.pallas import tpu as pltpu
from jax.sharding import PartitionSpec as P

MESH = pl.DeviceIdType.MESH
BF = jnp.bfloat16
F32 = jnp.float32
HD = 128
TOK = 256
HALF = 128


def dev(zh, x, c, zl, y):
    return (zh * 8 + x * 2 + c, zl * 8 + y)


def send(src, dst, ssem, rsem, to):
    pltpu.make_async_remote_copy(
        src_ref=src, dst_ref=dst, send_sem=ssem, recv_sem=rsem, device_id=to, device_id_type=MESH
    ).start()


def arrived(slot, sem):
    pltpu.make_async_copy(slot, slot, sem).wait()


def kernel(
    map_ref, q_ref, key_ref, val_ref, vturn_ref, bturn_ref, w_ref, out_ref,
    kv, q_all, score, top_ref, total_ref, acc_ref, wst, whop, w1, w2s, wfull, a_st, a_full, cst, cin,
    val_in, vturn_in, w_in, bturn_in, q_in, in_s,
    kc_s, kx_s, kx_r, kc_r, kd_s, kd_r, kxx_s, kxx_r,
    wh_s, wh_r, w1_s, w1_r, w2_s, w2_r, wx_s, wx_r, wd_s, wd_r,
    ac_s, ac_r, ring_s, rr_r, ll_r, c_s, c_r,
):
    s = lax.axis_index("seq")
    h = lax.axis_index("head")
    zh, x, c = s // 8, (s // 2) % 4, s % 2
    zl, y = h // 8, h % 8
    z = zh * 4 + zl

    g = zl * 2 + y // 4
    lanes = pl.ds(pl.multiple_of(g * HD, HD), HD)
    load_key = pltpu.make_async_copy(key_ref.at[:, lanes], kv.at[s, 0], in_s.at[0])
    load_val = pltpu.make_async_copy(val_ref.at[:, lanes], val_in, in_s.at[1])
    load_vturn = pltpu.make_async_copy(vturn_ref.at[g], vturn_in, in_s.at[2])
    load_w = pltpu.make_async_copy(w_ref, w_in, in_s.at[3])
    load_bturn = pltpu.make_async_copy(bturn_ref, bturn_in, in_s.at[4])
    load_q = pltpu.make_async_copy(q_ref, q_in, in_s.at[5])
    for load in (load_key, load_val, load_vturn, load_w, load_bturn, load_q):
        load.start()

    w_seq = zh * 8 + x * 2 + (y // 2) % 2
    w_at = zl * 2 + c

    def held_rows(xx, cc):
        hf = (xx + y // 4) % 2
        xs = (xx + 4 - hf) % 4
        return pl.multiple_of((2 * cc + xs // 2) * 256 + hf * 128, 128)

    rows = held_rows(x, c)

    def lanes1024(k):
        return pl.ds(pl.multiple_of(k * 1024, 1024), 1024)

    def row16(base, m):
        return pl.ds(pl.multiple_of(base + m * 16, 16), 16)

    def w1_place(n):
        hf, r, m = n // 16, (n // 8) % 2, n % 8
        return dev(zh, x, m % 2, m // 2, 4 * ((x + hf) % 2) + 2 * c + r)

    chunk = wfull.at[pl.ds(rows, 128), :]
    right = dev(zh, x, c, zl, (y + 1) % 8)
    left = dev(zh, x, c, zl, (y + 7) % 8)

    barrier = pltpu.get_barrier_semaphore()

    def greet(to):
        pl.semaphore_signal(barrier, inc=1, device_id=to, device_id_type=MESH)

    def greet_w1(hh, carry):
        @pl.when(jnp.logical_not((w_seq == s) & (hh == h)))
        def _():
            greet((w_seq, hh))

        return carry

    def entry():
        for d in range(1, 8):
            zt = (z + d) % 8
            greet(dev(zt // 4, x, c, zt % 4, y))
        for off in (1, 2, 3):
            greet(dev(zh, (x + off) % 4, c, zl, y))
        greet(dev(zh, x, 1 - c, zl, y))
        greet(right)
        greet(left)
        lax.fori_loop(0, 32, greet_w1, 0)
        for m in range(8):
            @pl.when(jnp.logical_not((c == zh) & (m == w_at)))
            def _():
                greet(dev(c, x, m % 2, m // 2, y))


    def all_in():
        own = (w_seq == s).astype(jnp.int32) + (c == zh).astype(jnp.int32)
        pl.semaphore_wait(barrier, 53 - own)

    def kv_first():
        load_key.wait()
        load_val.wait()
        load_vturn.wait()
        kv[s, 1] = jnp.dot(val_in[...], vturn_in[...], preferred_element_type=F32).astype(BF)

    def kv_send():
        @pl.when(zh == 0)
        def _():
            send(kv.at[s], kv.at[s], kc_s, kc_r, dev(1, x, c, zl, y))

        for off in (1, 2, 3):
            @pl.when(x + off < 4)
            def _():
                send(kv.at[s], kv.at[s], kx_s.at[off], kx_r.at[x], dev(zh, x + off, c, zl, y))

        send(kv.at[s], kv.at[s], kd_s.at[zh * 4 + x], kd_r.at[zh * 4 + x], dev(zh, x, 1 - c, zl, y))

    def w_turn(hf):
        if hf == 1:
            load_w.wait()
            load_bturn.wait()
        for i in range(4):
            for r in range(2):
                turned = lax.dot_general(
                    w_in[i * HD:(i + 1) * HD, (2 * r + hf) * 128:(2 * r + hf + 1) * 128], bturn_in[i],
                    (((0,), (1,)), ((), ())), preferred_element_type=F32,
                ).astype(BF)
                wst[hf * 16 + r * 8:hf * 16 + r * 8 + 8, i] = turned.reshape(8, 16, HD)

    def w_hop():
        far = wst.at[pl.ds(16, 16)]
        send(far, whop, wh_s, wh_r, dev(zh, (x + 1) % 4, c, zl, y))

    def w1_send(n, src):
        to = w1_place(n)
        mine = (to[0] == s) & (to[1] == h)

        @pl.when(jnp.logical_not(mine))
        def _():
            send(src, w1.at[pl.ds(h * 4, 4)], w1_s, w1_r, to)

        @pl.when(mine)
        def _():
            pltpu.make_async_copy(src, w1.at[pl.ds(h * 4, 4)], w1_r).start()

    def w_spread():
        def one(step, carry):
            n = (step + h) % 16
            w1_send(n, wst.at[n])
            return carry

        lax.fori_loop(0, 16, one, 0)

    def w_spread_far():
        arrived(whop, wh_r)

        def one(step, carry):
            n = (step + h) % 16
            w1_send(16 + n, whop.at[n])
            return carry

        lax.fori_loop(0, 16, one, 0)

    def kv_second():
        @pl.when(zh == 1)
        def _():
            arrived(kv.at[s - 8], kc_r)
            for off in (1, 3, 2):
                send(kv.at[s - 8], kv.at[s - 8], kxx_s.at[off], kxx_r.at[off], dev(1, (x + off) % 4, c, zl, y))
            send(kv.at[s - 8], kv.at[s - 8], kd_s.at[x], kd_r.at[x], dev(1, x, 1 - c, zl, y))

        for xs in range(3):
            @pl.when(xs < x)
            def _():
                slot = kv.at[zh * 8 + xs * 2 + c]
                arrived(slot, kx_r.at[xs])
                send(slot, slot, kd_s.at[zh * 4 + xs], kd_r.at[zh * 4 + xs], dev(zh, x, 1 - c, zl, y))

        @pl.when(zh == 1)
        def _():
            for off in (1, 3, 2):
                xs = (x + 4 - off) % 4
                slot = kv.at[xs * 2 + c]
                arrived(slot, kxx_r.at[off])
                send(slot, slot, kd_s.at[xs], kd_r.at[xs], dev(1, x, 1 - c, zl, y))

    def kv_wait():
        for xs in range(4):
            @pl.when(xs <= x)
            def _():
                arrived(kv.at[zh * 8 + xs * 2 + 1 - c], kd_r.at[zh * 4 + xs])

            @pl.when(zh == 1)
            def _():
                arrived(kv.at[xs * 2 + 1 - c], kd_r.at[xs])

    def w2_send(n, carry):
        k, step = n // 8, n % 8
        zt = (z + step) % 8
        zht, zlt = zt // 4, zt % 4
        for kk in range(8):
            block = map_ref[(zlt * 8 + k * 4 + kk // 2) * 4 + zht * 2 + kk % 2]
            w2s[k, step, :, kk * HD:(kk + 1) * HD] = w1[block]
        src = w2s.at[k, step]
        there = wfull.at[row16(held_rows(x, zh), w_at), lanes1024(k)]
        mine = (step == 0) & (c == zh)

        @pl.when(jnp.logical_not(mine))
        def _():
            send(src, there, w2_s, w2_r.at[k], dev(zht, x, zh, zlt, y))

        @pl.when(mine)
        def _():
            pltpu.make_async_copy(src, there, w2_r.at[k]).start()

        return carry

    def w_pick():
        arrived(w1, w1_r)
        lax.fori_loop(0, 16, w2_send, 0)

    def w_gather(k):
        piece = wfull.at[pl.ds(rows, 128), lanes1024(k)]
        arrived(piece, w2_r.at[k])
        for off in (1, 3):
            send(piece, piece, wx_s.at[off, k], wx_r.at[off, k], dev(zh, (x + off) % 4, c, zl, y))
        if k == 1:
            send(chunk, chunk, wd_s.at[0], wd_r.at[0], dev(zh, x, 1 - c, zl, y))

    def w_relay(off, k):
        base = held_rows((x + 4 - off) % 4, c)
        upper = wfull.at[pl.ds(base, 64), lanes1024(k)]
        lower = wfull.at[pl.ds(pl.multiple_of(base + 64, 64), 64), lanes1024(k)]
        if off == 2:
            arrived(upper, wx_r.at[2, k])
            arrived(lower, wx_r.at[0, k])
        else:
            arrived(wfull.at[pl.ds(base, 128), lanes1024(k)], wx_r.at[off, k])
            piece, kind = (upper, 2) if off == 1 else (lower, 0)
            send(piece, piece, wx_s.at[kind, k], wx_r.at[kind, k], dev(zh, (x + off) % 4, c, zl, y))
        if k == 1:
            theirs = wfull.at[pl.ds(base, 128), :]
            send(theirs, theirs, wd_s.at[off], wd_r.at[off], dev(zh, x, 1 - c, zl, y))

    def w_shared(off):
        base = held_rows((x + 4 - off) % 4, 1 - c)
        arrived(wfull.at[pl.ds(base, 128), :], wd_r.at[off])

    turn = math.log2(math.e) / math.sqrt(HD)
    last = zh * 4 + x

    def attention(t):
        def scored(i, u, j):
            return lax.dot_general(
                q_all[t, i], kv[2 * u + j, 0], (((1,), (1,)), ((), ())), preferred_element_type=F32
            )

        if t == 0:
            load_q.wait()
        for i in range(4):
            q_all[t, i] = q_in[t * HALF:(t + 1) * HALF, i * HD:(i + 1) * HD]
        place = lax.broadcasted_iota(jnp.int32, (HALF, TOK), 0) + (c * TOK + t * HALF)
        key_at = lax.broadcasted_iota(jnp.int32, (HALF, TOK), 1)
        for i in range(4):
            top = None
            for j in range(2):
                value = jnp.where(key_at + j * TOK <= place, scored(i, last, j), F32(-1e30))
                score[last, i, :, j * TOK:(j + 1) * TOK] = value
                value = jnp.maximum(value[:, :HD], value[:, HD:])
                top = value if top is None else jnp.maximum(top, value)
            top_ref[i] = top

        def first(u, carry):
            for i in range(4):
                top = top_ref[i]
                for j in range(2):
                    value = scored(i, u, j)
                    score[u, i, :, j * TOK:(j + 1) * TOK] = value
                    top = jnp.maximum(top, jnp.maximum(value[:, :HD], value[:, HD:]))
                top_ref[i] = top
            return carry

        lax.fori_loop(0, last, first, 0)
        for i in range(4):
            top_ref[i] = jnp.broadcast_to(jnp.max(top_ref[i], axis=1, keepdims=True) * turn, (HALF, HD))
        total_ref[...] = jnp.zeros_like(total_ref)
        acc_ref[...] = jnp.zeros_like(acc_ref)

        def second(u, carry):
            for i in range(4):
                top = top_ref[i]
                total = total_ref[i]
                acc = acc_ref[i]
                for j in range(2):
                    weight = []
                    for k in range(2):
                        lane = j * TOK + k * HD
                        weight.append(jnp.exp2(score[u, i, :, lane:lane + HD] * turn - top))
                        total = total + weight[k]
                    acc = acc + jnp.dot(
                        jnp.concatenate(weight, axis=1).astype(BF), kv[2 * u + j, 1], preferred_element_type=F32
                    )
                total_ref[i] = total
                acc_ref[i] = acc
            return carry

        lax.fori_loop(0, last + 1, second, 0)

        def head(i):
            return (acc_ref[i] / jnp.sum(total_ref[i], axis=1, keepdims=True)).astype(BF)

        for k in range(2):
            @pl.when(zh == k)
            def _():
                for i in range(2):
                    a_full[t, y, zh, :, i * HD:(i + 1) * HD] = head(2 * k + i)
                    a_st[t, :, i * HD:(i + 1) * HD] = head(2 * (1 - k) + i)

    def part(t, slot, p):
        return a_full.at[t, slot % 8, zh if p == 0 else 1 - zh]

    def go(t, k, p):
        if k < 3 or p == 0:
            ref = part(t, y + 8 - k, p)
            send(ref, ref, ring_s.at[t], rr_r.at[t, k, p], right)
        if k < 3 or p == 1:
            ref = part(t, y + k, p)
            send(ref, ref, ring_s.at[t], ll_r.at[t, k, p], left)

    def a_start(t):
        send(a_st.at[t], a_full.at[t, y, zh], ac_s.at[t], ac_r.at[t], dev(1 - zh, x, c, zl, y))
        go(t, 0, 0)

    def a_cross(t):
        arrived(part(t, y, 1), ac_r.at[t])
        go(t, 0, 1)

    def a_ring(t, k):
        for p in (0, 1):
            arrived(part(t, y + 8 - k, p), rr_r.at[t, k - 1, p])
            arrived(part(t, y + k, p), ll_r.at[t, k - 1, p])
            go(t, k, p)

    def a_last(t):
        arrived(part(t, y + 4, 0), rr_r.at[t, 3, 0])
        arrived(part(t, y + 4, 1), ll_r.at[t, 3, 1])

    def owner(off, cc):
        base = held_rows((x + 4 - off) % 4, cc)
        return base, base // 256, (base // 128) % 2

    def project(t, off):
        for cc in range(2):
            base, zlt, hf = owner(off, cc)
            acc = jnp.zeros((128, TOK), F32)
            for yy in range(8):
                acc = acc + lax.dot_general(
                    wfull[pl.ds(base, 128), yy * 256:(yy + 1) * 256], a_full[t, yy].reshape(TOK, 256),
                    (((1,), (1,)), ((), ())), preferred_element_type=F32,
                )
            for zht in range(2):
                value = acc[:, zht * HALF:(zht + 1) * HALF].astype(BF)
                mine = (zht == zh) & (zlt == zl)

                @pl.when(mine)
                def _():
                    cin[t, z, hf] = value

                @pl.when(jnp.logical_not(mine))
                def _():
                    piece = cst.at[t, off * 4 + cc * 2 + zht]
                    piece[...] = value
                    send(piece, cin.at[t, z, hf], c_s.at[t], c_r.at[t, z], dev(zht, x, c, zlt, y))

    def collect(t):
        for d in (1, 7, 2, 6, 3, 5, 4):
            zs = (z + d) % 8
            arrived(cin.at[t, zs], c_r.at[t, zs])
        for hf in range(2):
            total = cin[t, 0, hf].astype(F32)
            for zs in range(1, 8):
                total = total + cin[t, zs, hf].astype(F32)
            out_ref[hf * 128:(hf + 1) * 128, t * HALF:(t + 1) * HALF] = total.astype(BF)

    def kv_drain():
        @pl.when(zh == 0)
        def _():
            arrived(kv.at[s], kc_s)

        for off in (1, 2, 3):
            @pl.when(x + off < 4)
            def _():
                arrived(kv.at[s], kx_s.at[off])

            @pl.when(zh == 1)
            def _():
                arrived(kv.at[s], kxx_s.at[off])

        for xs in range(4):
            @pl.when(xs <= x)
            def _():
                arrived(kv.at[s], kd_s.at[zh * 4 + xs])

            @pl.when(zh == 1)
            def _():
                arrived(kv.at[s], kd_s.at[xs])

    def w_turn_drain():
        @pl.when(w_seq == s)
        def _():
            arrived(wst.at[pl.ds(0, 31)], w1_s)

        @pl.when(w_seq != s)
        def _():
            arrived(wst, w1_s)

    def w_pick_drain():
        arrived(whop, wh_s)
        @pl.when(c != zh)
        def _():
            arrived(w2s, w2_s)

        @pl.when(c == zh)
        def _():
            arrived(w2s.at[:, pl.ds(0, 7)], w2_s)

    def w_gather_drain():
        for off in range(4):
            for k in range(2):
                arrived(wfull.at[pl.ds(rows, 128 if off % 2 else 64), lanes1024(k)], wx_s.at[off, k])
            arrived(chunk, wd_s.at[off])

    def a_drain():
        for t in range(2):
            arrived(a_st.at[t], ac_s.at[t])
            arrived(a_full.at[t, pl.ds(0, 7)], ring_s.at[t])

    def proj_drain():
        for t in range(2):
            arrived(cst.at[t, pl.ds(0, 14)], c_s.at[t])

    entry()
    kv_first()
    all_in()
    kv_send()
    w_turn(1)
    w_hop()
    w_turn(0)
    kv_second()
    w_spread()
    w_spread_far()
    kv_wait()
    attention(0)
    a_start(0)
    attention(1)
    a_start(1)
    a_cross(0)
    w_pick()
    a_ring(0, 1)
    a_cross(1)
    a_ring(0, 2)
    w_gather(0)
    a_ring(1, 1)
    w_gather(1)
    a_ring(0, 3)
    w_relay(1, 0)
    w_relay(3, 0)
    a_ring(1, 2)
    a_last(0)
    w_shared(0)
    project(0, 0)
    w_relay(1, 1)
    w_relay(3, 1)
    a_ring(1, 3)
    w_shared(1)
    project(0, 1)
    w_shared(3)
    project(0, 3)
    a_last(1)
    project(1, 0)
    project(1, 1)
    project(1, 3)
    w_relay(2, 0)
    w_relay(2, 1)
    w_shared(2)
    project(0, 2)
    project(1, 2)
    kv_drain()
    w_turn_drain()
    w_pick_drain()
    w_gather_drain()
    a_drain()
    collect(0)
    collect(1)
    proj_drain()


def on_device(queries, key_rows, value_rows, value_turn, block_map, block_turn, out_weight):
    dma = pltpu.SemaphoreType.DMA
    return pl.pallas_call(
        kernel,
        out_shape=jax.ShapeDtypeStruct((256, TOK), BF),
        in_specs=[pl.BlockSpec(memory_space=pltpu.SMEM)] + [pl.BlockSpec(memory_space=pltpu.HBM)] * 6,
        out_specs=pl.BlockSpec(memory_space=pltpu.VMEM),
        scratch_shapes=[
            pltpu.VMEM((16, 2, TOK, HD), BF),
            pltpu.VMEM((2, 4, HALF, HD), BF),
            pltpu.VMEM((8, 4, HALF, 2 * TOK), F32),
            pltpu.VMEM((4, HALF, HD), F32),
            pltpu.VMEM((4, HALF, HD), F32),
            pltpu.VMEM((4, HALF, HD), F32),
            pltpu.VMEM((32, 4, 16, HD), BF),
            pltpu.VMEM((16, 4, 16, HD), BF),
            pltpu.VMEM((128, 16, HD), BF),
            pltpu.VMEM((2, 8, 16, 1024), BF),
            pltpu.VMEM((1024, 2048), BF),
            pltpu.VMEM((2, HALF, 256), BF),
            pltpu.VMEM((2, 8, 2, HALF, 256), BF),
            pltpu.VMEM((2, 16, 128, HALF), BF),
            pltpu.VMEM((2, 8, 2, 128, HALF), BF),
            pltpu.VMEM((TOK, HD), BF),
            pltpu.VMEM((HD, HD), BF),
            pltpu.VMEM((512, 512), BF),
            pltpu.VMEM((4, HD, HD), BF),
            pltpu.VMEM((TOK, 512), BF),
            dma((6,)),
            dma(()), dma((4,)), dma((4,)), dma(()), dma((8,)), dma((8,)), dma((4,)), dma((4,)),
            dma(()), dma(()), dma(()), dma(()), dma(()), dma((2,)), dma((4, 2)), dma((4, 2)), dma((4,)), dma((4,)),
            dma((2,)), dma((2,)), dma((2,)), dma((2, 4, 2)), dma((2, 4, 2)), dma((2,)), dma((2, 8)),
        ],
        compiler_params=pltpu.CompilerParams(
            has_side_effects=True, collective_id=0, vmem_limit_bytes=60 * 1024 * 1024
        ),
    )(block_map, queries, key_rows, value_rows, value_turn, block_turn, out_weight)


def solution(mesh):
    placed = (
        P("seq", "head"),
        P("seq", None),
        P("seq", None),
        P(),
        P(),
        P("head", None, None),
        P("head", "seq"),
    )
    return jax.shard_map(
        on_device, mesh=mesh, in_specs=placed, out_specs=P("head", "seq"), check_vma=False
    )
```

```python
import math

import jax
import jax.numpy as jnp
from jax import lax
from jax.experimental import pallas as pl
from jax.experimental.pallas import tpu as pltpu
from jax.sharding import PartitionSpec as P

MESH = pl.DeviceIdType.MESH
BF = jnp.bfloat16
F32 = jnp.float32
HD = 128
TOK = 256
HALF = 128


def dev(zh, x, c, zl, y):
    return (zh * 8 + x * 2 + c, zl * 8 + y)


def send(src, dst, ssem, rsem, to):
    pltpu.make_async_remote_copy(
        src_ref=src, dst_ref=dst, send_sem=ssem, recv_sem=rsem, device_id=to, device_id_type=MESH
    ).start()


def arrived(slot, sem):
    pltpu.make_async_copy(slot, slot, sem).wait()


def kernel(
    map_ref, q_ref, key_ref, val_ref, vturn_ref, bturn_ref, w_ref, out_ref,
    kv, q_all, score, top_ref, total_ref, acc_ref, wst, whop, w1, w2s, wfull, a_st, a_full, cst, cin,
    val_in, vturn_in, w_in, bturn_in, q_in, in_s,
    kc_s, kx_s, kx_r, kc_r, kd_s, kd_r, kxx_s, kxx_r,
    wh_s, wh_r, w1_s, w1_r, w2_s, w2_r, wx_s, wx_r, wd_s, wd_r,
    ac_s, ac_r, ring_s, rr_r, ll_r, c_s, c_r,
):
    s = lax.axis_index("seq")
    h = lax.axis_index("head")
    zh, x, c = s // 8, (s // 2) % 4, s % 2
    zl, y = h // 8, h % 8
    z = zh * 4 + zl

    g = zl * 2 + y // 4
    lanes = pl.ds(pl.multiple_of(g * HD, HD), HD)
    load_key = pltpu.make_async_copy(key_ref.at[:, lanes], kv.at[s, 0], in_s.at[0])
    load_val = pltpu.make_async_copy(val_ref.at[:, lanes], val_in, in_s.at[1])
    load_vturn = pltpu.make_async_copy(vturn_ref.at[g], vturn_in, in_s.at[2])
    load_w = pltpu.make_async_copy(w_ref, w_in, in_s.at[3])
    load_bturn = pltpu.make_async_copy(bturn_ref, bturn_in, in_s.at[4])
    load_q = pltpu.make_async_copy(q_ref, q_in, in_s.at[5])

    w_seq = zh * 8 + x * 2 + (y // 2) % 2
    w_at = zl * 2 + c

    def held_rows(xx, cc):
        hf = (xx + y // 4) % 2
        xs = (xx + 4 - hf) % 4
        return pl.multiple_of((2 * cc + xs // 2) * 256 + hf * 128, 128)

    rows = held_rows(x, c)

    def lanes1024(k):
        return pl.ds(pl.multiple_of(k * 1024, 1024), 1024)

    def row16(base, m):
        return pl.ds(pl.multiple_of(base + m * 16, 16), 16)

    def w1_place(n):
        hf, r, m = n // 16, (n // 8) % 2, n % 8
        return dev(zh, x, m % 2, m // 2, 4 * ((x + hf) % 2) + 2 * c + r)

    chunk = wfull.at[pl.ds(rows, 128), :]
    right = dev(zh, x, c, zl, (y + 1) % 8)
    left = dev(zh, x, c, zl, (y + 7) % 8)

    barrier = pltpu.get_barrier_semaphore()

    def greet(to):
        pl.semaphore_signal(barrier, inc=1, device_id=to, device_id_type=MESH)

    def greet_w1(hh, carry):
        @pl.when(jnp.logical_not((w_seq == s) & (hh == h)))
        def _():
            greet((w_seq, hh))

        return carry

    def entry():
        for d in range(1, 8):
            zt = (z + d) % 8
            greet(dev(zt // 4, x, c, zt % 4, y))
        for off in (1, 2, 3):
            greet(dev(zh, (x + off) % 4, c, zl, y))
        greet(dev(zh, x, 1 - c, zl, y))
        greet(right)
        greet(left)
        lax.fori_loop(0, 32, greet_w1, 0)
        for m in range(8):
            @pl.when(jnp.logical_not((c == zh) & (m == w_at)))
            def _():
                greet(dev(c, x, m % 2, m // 2, y))


    def all_in():
        own = (w_seq == s).astype(jnp.int32) + (c == zh).astype(jnp.int32)
        pl.semaphore_wait(barrier, 53 - own)

    def kv_first():
        load_key.wait()
        load_val.wait()
        load_vturn.wait()
        kv[s, 1] = jnp.dot(val_in[...], vturn_in[...], preferred_element_type=F32).astype(BF)

    def kv_send():
        @pl.when(zh == 0)
        def _():
            send(kv.at[s], kv.at[s], kc_s, kc_r, dev(1, x, c, zl, y))

        for off in (1, 2, 3):
            @pl.when(x + off < 4)
            def _():
                send(kv.at[s], kv.at[s], kx_s.at[off], kx_r.at[x], dev(zh, x + off, c, zl, y))

        send(kv.at[s], kv.at[s], kd_s.at[zh * 4 + x], kd_r.at[zh * 4 + x], dev(zh, x, 1 - c, zl, y))

    def w_turn(hf):
        if hf == 1:
            load_w.wait()
            load_bturn.wait()
        for i in range(4):
            for r in range(2):
                turned = lax.dot_general(
                    w_in[i * HD:(i + 1) * HD, (2 * r + hf) * 128:(2 * r + hf + 1) * 128], bturn_in[i],
                    (((0,), (1,)), ((), ())), preferred_element_type=F32,
                ).astype(BF)
                wst[hf * 16 + r * 8:hf * 16 + r * 8 + 8, i] = turned.reshape(8, 16, HD)

    def w_hop():
        far = wst.at[pl.ds(16, 16)]
        send(far, whop, wh_s, wh_r, dev(zh, (x + 1) % 4, c, zl, y))

    def w1_send(n, src):
        to = w1_place(n)
        mine = (to[0] == s) & (to[1] == h)

        @pl.when(jnp.logical_not(mine))
        def _():
            send(src, w1.at[pl.ds(h * 4, 4)], w1_s, w1_r, to)

        @pl.when(mine)
        def _():
            pltpu.make_async_copy(src, w1.at[pl.ds(h * 4, 4)], w1_r).start()

    def w_spread():
        def one(step, carry):
            n = (step + h) % 16
            w1_send(n, wst.at[n])
            return carry

        lax.fori_loop(0, 16, one, 0)

    def w_spread_far():
        arrived(whop, wh_r)

        def one(step, carry):
            n = (step + h) % 16
            w1_send(16 + n, whop.at[n])
            return carry

        lax.fori_loop(0, 16, one, 0)

    def kv_second():
        @pl.when(zh == 1)
        def _():
            arrived(kv.at[s - 8], kc_r)
            for off in (1, 3, 2):
                send(kv.at[s - 8], kv.at[s - 8], kxx_s.at[off], kxx_r.at[off], dev(1, (x + off) % 4, c, zl, y))
            send(kv.at[s - 8], kv.at[s - 8], kd_s.at[x], kd_r.at[x], dev(1, x, 1 - c, zl, y))

        for xs in range(3):
            @pl.when(xs < x)
            def _():
                slot = kv.at[zh * 8 + xs * 2 + c]
                arrived(slot, kx_r.at[xs])
                send(slot, slot, kd_s.at[zh * 4 + xs], kd_r.at[zh * 4 + xs], dev(zh, x, 1 - c, zl, y))

        @pl.when(zh == 1)
        def _():
            for off in (1, 3, 2):
                xs = (x + 4 - off) % 4
                slot = kv.at[xs * 2 + c]
                arrived(slot, kxx_r.at[off])
                send(slot, slot, kd_s.at[xs], kd_r.at[xs], dev(1, x, 1 - c, zl, y))

    def kv_wait():
        for xs in range(4):
            @pl.when(xs <= x)
            def _():
                arrived(kv.at[zh * 8 + xs * 2 + 1 - c], kd_r.at[zh * 4 + xs])

            @pl.when(zh == 1)
            def _():
                arrived(kv.at[xs * 2 + 1 - c], kd_r.at[xs])

    def w2_send(n, carry):
        k, turn_at = n // 8, n % 8
        far = (turn_at + 1) // 2
        step = jnp.where(turn_at % 2 == 1, 4 + far, 12 - far) % 8
        zt = (z + step) % 8
        zht, zlt = zt // 4, zt % 4
        for kk in range(8):
            block = map_ref[(zlt * 8 + k * 4 + kk // 2) * 4 + zht * 2 + kk % 2]
            w2s[k, step, :, kk * HD:(kk + 1) * HD] = w1[block]
        src = w2s.at[k, step]
        there = wfull.at[row16(held_rows(x, zh), w_at), lanes1024(k)]
        mine = (step == 0) & (c == zh)

        @pl.when(jnp.logical_not(mine))
        def _():
            send(src, there, w2_s, w2_r.at[k], dev(zht, x, zh, zlt, y))

        @pl.when(mine)
        def _():
            pltpu.make_async_copy(src, there, w2_r.at[k]).start()

        return carry

    def w_pick():
        arrived(w1, w1_r)
        lax.fori_loop(0, 16, w2_send, 0)

    def w_gather(k):
        piece = wfull.at[pl.ds(rows, 128), lanes1024(k)]
        arrived(piece, w2_r.at[k])
        for off in (1, 3):
            send(piece, piece, wx_s.at[off, k], wx_r.at[off, k], dev(zh, (x + off) % 4, c, zl, y))
        if k == 1:
            send(chunk, chunk, wd_s.at[0], wd_r.at[0], dev(zh, x, 1 - c, zl, y))

    def w_relay(off, k):
        base = held_rows((x + 4 - off) % 4, c)
        upper = wfull.at[pl.ds(base, 64), lanes1024(k)]
        lower = wfull.at[pl.ds(pl.multiple_of(base + 64, 64), 64), lanes1024(k)]
        if off == 2:
            arrived(upper, wx_r.at[2, k])
            arrived(lower, wx_r.at[0, k])
        else:
            arrived(wfull.at[pl.ds(base, 128), lanes1024(k)], wx_r.at[off, k])
            piece, kind = (upper, 2) if off == 1 else (lower, 0)
            send(piece, piece, wx_s.at[kind, k], wx_r.at[kind, k], dev(zh, (x + off) % 4, c, zl, y))
        if k == 1:
            theirs = wfull.at[pl.ds(base, 128), :]
            send(theirs, theirs, wd_s.at[off], wd_r.at[off], dev(zh, x, 1 - c, zl, y))

    def w_shared(off):
        base = held_rows((x + 4 - off) % 4, 1 - c)
        arrived(wfull.at[pl.ds(base, 128), :], wd_r.at[off])

    turn = math.log2(math.e) / math.sqrt(HD)
    last = zh * 4 + x

    def attention(t):
        def scored(i, u, j):
            return lax.dot_general(
                q_all[t, i], kv[2 * u + j, 0], (((1,), (1,)), ((), ())), preferred_element_type=F32
            )

        if t == 0:
            load_q.wait()
        for i in range(4):
            q_all[t, i] = q_in[t * HALF:(t + 1) * HALF, i * HD:(i + 1) * HD]
        place = lax.broadcasted_iota(jnp.int32, (HALF, TOK), 0) + (c * TOK + t * HALF)
        key_at = lax.broadcasted_iota(jnp.int32, (HALF, TOK), 1)
        for i in range(4):
            top = None
            for j in range(2):
                value = jnp.where(key_at + j * TOK <= place, scored(i, last, j), F32(-1e30))
                score[last, i, :, j * TOK:(j + 1) * TOK] = value
                value = jnp.maximum(value[:, :HD], value[:, HD:])
                top = value if top is None else jnp.maximum(top, value)
            top_ref[i] = top

        def first(u, carry):
            for i in range(4):
                top = top_ref[i]
                for j in range(2):
                    value = scored(i, u, j)
                    score[u, i, :, j * TOK:(j + 1) * TOK] = value
                    top = jnp.maximum(top, jnp.maximum(value[:, :HD], value[:, HD:]))
                top_ref[i] = top
            return carry

        lax.fori_loop(0, last, first, 0)
        for i in range(4):
            top_ref[i] = jnp.broadcast_to(jnp.max(top_ref[i], axis=1, keepdims=True) * turn, (HALF, HD))
        total_ref[...] = jnp.zeros_like(total_ref)
        acc_ref[...] = jnp.zeros_like(acc_ref)

        def second(u, carry):
            for i in range(4):
                top = top_ref[i]
                total = total_ref[i]
                acc = acc_ref[i]
                for j in range(2):
                    weight = []
                    for k in range(2):
                        lane = j * TOK + k * HD
                        weight.append(jnp.exp2(score[u, i, :, lane:lane + HD] * turn - top))
                        total = total + weight[k]
                    acc = acc + jnp.dot(
                        jnp.concatenate(weight, axis=1).astype(BF), kv[2 * u + j, 1], preferred_element_type=F32
                    )
                total_ref[i] = total
                acc_ref[i] = acc
            return carry

        lax.fori_loop(0, last + 1, second, 0)

        def head(i):
            return (acc_ref[i] / jnp.sum(total_ref[i], axis=1, keepdims=True)).astype(BF)

        for k in range(2):
            @pl.when(zh == k)
            def _():
                for i in range(2):
                    a_full[t, y, zh, :, i * HD:(i + 1) * HD] = head(2 * k + i)
                    a_st[t, :, i * HD:(i + 1) * HD] = head(2 * (1 - k) + i)

    def part(t, slot, p):
        return a_full.at[t, slot % 8, zh if p == 0 else 1 - zh]

    def go(t, k, p):
        if k < 3 or p == 0:
            ref = part(t, y + 8 - k, p)
            send(ref, ref, ring_s.at[t], rr_r.at[t, k, p], right)
        if k < 3 or p == 1:
            ref = part(t, y + k, p)
            send(ref, ref, ring_s.at[t], ll_r.at[t, k, p], left)

    def a_start(t):
        send(a_st.at[t], a_full.at[t, y, zh], ac_s.at[t], ac_r.at[t], dev(1 - zh, x, c, zl, y))
        go(t, 0, 0)

    def a_cross(t):
        arrived(part(t, y, 1), ac_r.at[t])
        go(t, 0, 1)

    def a_ring(t, k):
        for p in (0, 1):
            arrived(part(t, y + 8 - k, p), rr_r.at[t, k - 1, p])
            arrived(part(t, y + k, p), ll_r.at[t, k - 1, p])
            go(t, k, p)

    def a_last(t):
        arrived(part(t, y + 4, 0), rr_r.at[t, 3, 0])
        arrived(part(t, y + 4, 1), ll_r.at[t, 3, 1])

    def owner(off, cc):
        base = held_rows((x + 4 - off) % 4, cc)
        return base, base // 256, (base // 128) % 2

    def project(t, off):
        for cc in range(2):
            base, zlt, hf = owner(off, cc)
            acc = jnp.zeros((128, TOK), F32)
            for yy in range(8):
                acc = acc + lax.dot_general(
                    wfull[pl.ds(base, 128), yy * 256:(yy + 1) * 256], a_full[t, yy].reshape(TOK, 256),
                    (((1,), (1,)), ((), ())), preferred_element_type=F32,
                )
            for zht in range(2):
                value = acc[:, zht * HALF:(zht + 1) * HALF].astype(BF)
                mine = (zht == zh) & (zlt == zl)

                @pl.when(mine)
                def _():
                    cin[t, z, hf] = value

                @pl.when(jnp.logical_not(mine))
                def _():
                    piece = cst.at[t, off * 4 + cc * 2 + zht]
                    piece[...] = value
                    send(piece, cin.at[t, z, hf], c_s.at[t], c_r.at[t, z], dev(zht, x, c, zlt, y))

    def collect(t):
        for d in (1, 7, 2, 6, 3, 5, 4):
            zs = (z + d) % 8
            arrived(cin.at[t, zs], c_r.at[t, zs])
        for hf in range(2):
            total = cin[t, 0, hf].astype(F32)
            for zs in range(1, 8):
                total = total + cin[t, zs, hf].astype(F32)
            out_ref[hf * 128:(hf + 1) * 128, t * HALF:(t + 1) * HALF] = total.astype(BF)

    def kv_drain():
        @pl.when(zh == 0)
        def _():
            arrived(kv.at[s], kc_s)

        for off in (1, 2, 3):
            @pl.when(x + off < 4)
            def _():
                arrived(kv.at[s], kx_s.at[off])

            @pl.when(zh == 1)
            def _():
                arrived(kv.at[s], kxx_s.at[off])

        for xs in range(4):
            @pl.when(xs <= x)
            def _():
                arrived(kv.at[s], kd_s.at[zh * 4 + xs])

            @pl.when(zh == 1)
            def _():
                arrived(kv.at[s], kd_s.at[xs])

    def w_turn_drain():
        @pl.when(w_seq == s)
        def _():
            arrived(wst.at[pl.ds(0, 31)], w1_s)

        @pl.when(w_seq != s)
        def _():
            arrived(wst, w1_s)

    def w_pick_drain():
        arrived(whop, wh_s)
        @pl.when(c != zh)
        def _():
            arrived(w2s, w2_s)

        @pl.when(c == zh)
        def _():
            arrived(w2s.at[:, pl.ds(0, 7)], w2_s)

    def w_gather_drain():
        for off in range(4):
            for k in range(2):
                arrived(wfull.at[pl.ds(rows, 128 if off % 2 else 64), lanes1024(k)], wx_s.at[off, k])
            arrived(chunk, wd_s.at[off])

    def a_drain():
        for t in range(2):
            arrived(a_st.at[t], ac_s.at[t])
            arrived(a_full.at[t, pl.ds(0, 7)], ring_s.at[t])

    def proj_drain():
        for t in range(2):
            arrived(cst.at[t, pl.ds(0, 14)], c_s.at[t])

    entry()
    for load in (load_key, load_val, load_vturn, load_w, load_bturn, load_q):
        load.start()
    kv_first()
    all_in()
    kv_send()
    w_turn(1)
    w_hop()
    w_turn(0)
    kv_second()
    w_spread()
    w_spread_far()
    kv_wait()
    attention(0)
    a_start(0)
    attention(1)
    a_start(1)
    a_cross(0)
    w_pick()
    a_ring(0, 1)
    a_cross(1)
    a_ring(0, 2)
    w_gather(0)
    a_ring(1, 1)
    w_gather(1)
    a_ring(0, 3)
    w_relay(1, 0)
    w_relay(3, 0)
    a_ring(1, 2)
    a_last(0)
    w_shared(0)
    project(0, 0)
    w_relay(1, 1)
    w_relay(3, 1)
    a_ring(1, 3)
    w_shared(1)
    project(0, 1)
    w_shared(3)
    project(0, 3)
    a_last(1)
    project(1, 0)
    project(1, 1)
    project(1, 3)
    w_relay(2, 0)
    w_relay(2, 1)
    w_shared(2)
    project(0, 2)
    project(1, 2)
    kv_drain()
    w_turn_drain()
    w_pick_drain()
    w_gather_drain()
    a_drain()
    collect(0)
    collect(1)
    proj_drain()


def on_device(queries, key_rows, value_rows, value_turn, block_map, block_turn, out_weight):
    dma = pltpu.SemaphoreType.DMA
    return pl.pallas_call(
        kernel,
        out_shape=jax.ShapeDtypeStruct((256, TOK), BF),
        in_specs=[pl.BlockSpec(memory_space=pltpu.SMEM)] + [pl.BlockSpec(memory_space=pltpu.HBM)] * 6,
        out_specs=pl.BlockSpec(memory_space=pltpu.VMEM),
        scratch_shapes=[
            pltpu.VMEM((16, 2, TOK, HD), BF),
            pltpu.VMEM((2, 4, HALF, HD), BF),
            pltpu.VMEM((8, 4, HALF, 2 * TOK), F32),
            pltpu.VMEM((4, HALF, HD), F32),
            pltpu.VMEM((4, HALF, HD), F32),
            pltpu.VMEM((4, HALF, HD), F32),
            pltpu.VMEM((32, 4, 16, HD), BF),
            pltpu.VMEM((16, 4, 16, HD), BF),
            pltpu.VMEM((128, 16, HD), BF),
            pltpu.VMEM((2, 8, 16, 1024), BF),
            pltpu.VMEM((1024, 2048), BF),
            pltpu.VMEM((2, HALF, 256), BF),
            pltpu.VMEM((2, 8, 2, HALF, 256), BF),
            pltpu.VMEM((2, 16, 128, HALF), BF),
            pltpu.VMEM((2, 8, 2, 128, HALF), BF),
            pltpu.VMEM((TOK, HD), BF),
            pltpu.VMEM((HD, HD), BF),
            pltpu.VMEM((512, 512), BF),
            pltpu.VMEM((4, HD, HD), BF),
            pltpu.VMEM((TOK, 512), BF),
            dma((6,)),
            dma(()), dma((4,)), dma((4,)), dma(()), dma((8,)), dma((8,)), dma((4,)), dma((4,)),
            dma(()), dma(()), dma(()), dma(()), dma(()), dma((2,)), dma((4, 2)), dma((4, 2)), dma((4,)), dma((4,)),
            dma((2,)), dma((2,)), dma((2,)), dma((2, 4, 2)), dma((2, 4, 2)), dma((2,)), dma((2, 8)),
        ],
        compiler_params=pltpu.CompilerParams(
            has_side_effects=True, collective_id=0, vmem_limit_bytes=60 * 1024 * 1024
        ),
    )(block_map, queries, key_rows, value_rows, value_turn, block_turn, out_weight)


def solution(mesh):
    placed = (
        P("seq", "head"),
        P("seq", None),
        P("seq", None),
        P(),
        P(),
        P("head", None, None),
        P("head", "seq"),
    )
    return jax.shard_map(
        on_device, mesh=mesh, in_specs=placed, out_specs=P("head", "seq"), check_vma=False
    )
```
